32 devices in a mesh: fsdp: 8 (over y, x, core), tp: 4 (over z).
Axes of the slice: x: 2, y: 2, z: 4, core: 2. Of those that a mesh axis runs over, the one named last changes fastest.
Arguments:
- activations: bfloat16 [8, 2048, 1152], P('fsdp', 'tp'), may hold values from -6 to 6
- lengths: int32 [8, 3], P('fsdp'), may hold values from 100 to 1024, as said below
- cotangent: bfloat16 [8, 2048, 1152], P('fsdp', 'tp'), may hold values from -6 to 6
- ln1_gain: float32 [1, 1152], P(None, 'fsdp'), may hold values from 0.5 to 1.5
- ln1_bias: float32 [1, 1152], P(None, 'fsdp'), may hold values from -2 to 2
- query_weight: bfloat16 [1, 1152, 1152], P(None, 'fsdp', 'tp'), may hold values from -0.1875 to 0.1875
- query_bias: float32 [1, 1152], P(None, 'tp'), may hold values from -3 to 3
- key_weight: bfloat16 [1, 1152, 1152], P(None, 'fsdp', 'tp'), may hold values from -0.1875 to 0.1875
- value_weight: bfloat16 [1, 1152, 1152], P(None, 'fsdp', 'tp'), may hold values from -0.1875 to 0.1875
- value_bias: float32 [1, 1152], P(None, 'tp'), may hold values from -3 to 3
- out_weight: bfloat16 [1, 1152, 1152], P(None, 'fsdp', 'tp'), may hold values from -0.75 to 0.75
- out_bias: float32 [1, 1152], P(None, 'fsdp'), may hold values from -2 to 2
- ln2_gain: float32 [1, 1152], P(None, 'fsdp'), may hold values from 0.5 to 1.5
- ln2_bias: float32 [1, 1152], P(None, 'fsdp'), may hold values from -2 to 2
- up_weight: bfloat16 [1, 1152, 4304], P(None, 'fsdp', 'tp'), may hold values from -0.1875 to 0.1875
- up_bias: float32 [1, 4304], P(None, 'tp'), may hold values from -3 to 3
- down_weight: bfloat16 [1, 1152, 4304], P(None, 'fsdp', 'tp'), may hold values from -0.09375 to 0.09375
- down_bias: float32 [1, 1152], P(None, 'fsdp'), may hold values from -2 to 2
Outputs:
- activations_out: bfloat16 [8, 2048, 1152], P('fsdp', 'tp')
- input_grad: float32 [8, 2048, 1152], P('fsdp', 'tp')
- ln1_gain_grad: float32 [1, 1152], P(None, 'fsdp')
- ln1_bias_grad: float32 [1, 1152], P(None, 'fsdp')
- query_weight_grad: float32 [1, 1152, 1152], P(None, 'fsdp', 'tp')
- query_bias_grad: float32 [1, 1152], P(None, 'tp')
- key_weight_grad: float32 [1, 1152, 1152], P(None, 'fsdp', 'tp')
- value_weight_grad: float32 [1, 1152, 1152], P(None, 'fsdp', 'tp')
- value_bias_grad: float32 [1, 1152], P(None, 'tp')
- out_weight_grad: float32 [1, 1152, 1152], P(None, 'fsdp', 'tp')
- out_bias_grad: float32 [1, 1152], P(None, 'fsdp')
- ln2_gain_grad: float32 [1, 1152], P(None, 'fsdp')
- ln2_bias_grad: float32 [1, 1152], P(None, 'fsdp')
- up_weight_grad: float32 [1, 1152, 4304], P(None, 'fsdp', 'tp')
- up_bias_grad: float32 [1, 4304], P(None, 'tp')
- down_weight_grad: float32 [1, 1152, 4304], P(None, 'fsdp', 'tp')
- down_bias_grad: float32 [1, 1152], P(None, 'fsdp')
The draws below stay inside these ranges and needn't reach their ends.
Inputs may be any that keep to these rules, and one draw needn't show every extreme that they name: `lengths`: each row holds 3 pictures laid end to end from slot 0, each of 100 to 1024 patches and together at most 2048; the slots after them are padding; some row has a picture of exactly 1024 patches.
All inputs are finite; a program needn't handle non-finite values.
Results may differ from the reference program's by a relative error of at most 0.033.
Values may be sent and summed in bfloat16 or wider, within the bound.
No kernel may reach another device: no remote copies, remote signals or barrier semaphores. Data moves between devices by JAX's collectives and lax.ppermute only.
A program may use at most 192 MiB of HBM per device.

```python
from functools import partial
import jax
import jax.numpy as jnp
from jax import lax

D = 1152
HEADS = 16
HEAD_DIM = 72
FF = 4304
HH = 1152
LAYERS = 1
SLOTS = 2048
PICS = 3
PIC_MIN = 100
PIC_MAX = 1024
ROWS = 8


def draw_lengths(key, part):
    first_key, second_key, third_key, row_key = jax.random.split(key, 4)
    first = jax.random.randint(first_key, (ROWS,), PIC_MIN, PIC_MAX + 1)
    chosen = jax.random.randint(row_key, (), 0, ROWS)
    first = jnp.where(jnp.arange(ROWS) == chosen, PIC_MAX, first)
    second_top = jnp.minimum(PIC_MAX, SLOTS - first - PIC_MIN)
    second = jax.random.randint(second_key, (ROWS,), PIC_MIN, second_top + 1)
    third_top = jnp.minimum(PIC_MAX, SLOTS - first - second)
    third = jax.random.randint(third_key, (ROWS,), PIC_MIN, third_top + 1)
    return jnp.stack([first, second, third], axis=1).astype(jnp.int32)


def raised(result, rng, source, target, shards_of, factor):
    owner, partner = [(jnp.arange(result.shape[axis_at]) // (result.shape[axis_at] // shards_of)).reshape([-1 if axis == axis_at else 1 for axis in range(result.ndim)]) for axis_at in (source, target)]
    chosen = jax.random.permutation(rng, shards_of)[partner]
    strong = (owner == chosen) | (owner == (partner + shards_of // 2) % shards_of)
    return jnp.where(strong, factor * result, result)


def level_of(rng, dims, shards, low, largest):
    loudness = 1.0
    for axis_at, shards_of in shards:
        steps = jax.random.uniform(jax.random.fold_in(jax.random.fold_in(rng, 6), axis_at), (shards_of,), jnp.float32, low / len(shards), largest / len(shards))
        loudness = loudness * jnp.repeat(jnp.exp(steps), dims[axis_at] // shards_of).reshape((-1,) + (1,) * (len(dims) - 1 - axis_at))
    return loudness


def noise(rng, shape, scale, limit, cuts=(), kind=jnp.bfloat16):
    array = jax.random.normal(rng, shape, jnp.float32) * scale
    if len(cuts) > 0:
        array = level_of(rng, shape, cuts, -0.22, 0.18) * array
    return jnp.clip(array, min=-limit, max=limit).astype(kind)


def bell_draw_with(own_key, shape, deviation, limit, shards, heavy, kind=jnp.bfloat16):
    entries = deviation * jax.random.normal(own_key, shape, jnp.float32)
    if shards:
        entries = entries * level_of(own_key, shape, shards, -0.22, 0.18)
    return jnp.clip(raised(entries, jax.random.fold_in(own_key, 3), *heavy), -limit, limit).astype(kind)


def setup_inputs(seed: int = 0) -> dict:
    streams_of = jax.random.split(jax.random.key(seed), 19)
    activations = noise(streams_of[0], (ROWS, SLOTS, D), 1.0, 6.0, ((0, 8), (1, 4)))
    lengths = draw_lengths(jax.random.fold_in(streams_of[18], 71), 0)
    cotangent = bell_draw_with(streams_of[2], (ROWS, SLOTS, D), 1.0, 6.0, ((0, 8), (1, 4)), (0, 2, 8, 2.0))
    ln1_gain = jnp.clip(1.0 + 0.1 * jax.random.normal(streams_of[3], (LAYERS, D), jnp.float32), 0.5, 1.5)
    ln1_bias = noise(streams_of[4], (LAYERS, D), 0.3, 2.0, ((1, 8),), jnp.float32)
    query_weight = noise(streams_of[5], (LAYERS, D, HH), D ** -0.5, 0.1875, ((1, 8), (2, 4)))
    query_bias = noise(streams_of[6], (LAYERS, HH), 0.5, 3.0, ((1, 4),), jnp.float32)
    key_weight = noise(streams_of[7], (LAYERS, D, HH), D ** -0.5, 0.1875, ((1, 8), (2, 4)))
    value_weight = noise(streams_of[8], (LAYERS, D, HH), D ** -0.5, 0.1875, ((1, 8), (2, 4)))
    value_bias = noise(streams_of[9], (LAYERS, HH), 0.5, 3.0, ((1, 4),), jnp.float32)
    out_weight = noise(streams_of[10], (LAYERS, D, HH), (HH // 16) ** -0.5, 0.75, ((1, 8), (2, 4)))
    out_bias = noise(streams_of[11], (LAYERS, D), 0.3, 2.0, ((1, 8),), jnp.float32)
    ln2_gain = jnp.clip(1.0 + 0.1 * jax.random.normal(streams_of[12], (LAYERS, D), jnp.float32), 0.5, 1.5)
    ln2_bias = noise(streams_of[13], (LAYERS, D), 0.3, 2.0, ((1, 8),), jnp.float32)
    up_weight = noise(streams_of[14], (LAYERS, D, FF), D ** -0.5, 0.1875, ((1, 8), (2, 4)))
    up_bias = noise(streams_of[15], (LAYERS, FF), 0.5, 3.0, ((1, 4),), jnp.float32)
    down_weight = noise(streams_of[16], (LAYERS, D, FF), FF ** -0.5, 0.09375, ((1, 8), (2, 4)))
    down_bias = noise(streams_of[17], (LAYERS, D), 0.3, 2.0, ((1, 8),), jnp.float32)
    return {"activations": activations, "lengths": lengths, "cotangent": cotangent, "ln1_gain": ln1_gain, "ln1_bias": ln1_bias, "query_weight": query_weight, "query_bias": query_bias, "key_weight": key_weight, "value_weight": value_weight, "value_bias": value_bias, "out_weight": out_weight, "out_bias": out_bias, "ln2_gain": ln2_gain, "ln2_bias": ln2_bias, "up_weight": up_weight, "up_bias": up_bias, "down_weight": down_weight, "down_bias": down_bias}


highest_mode = lax.Precision.HIGHEST

@jax.custom_vjp
def low(v):
    return lax.optimization_barrier(v.astype(jnp.bfloat16)).astype(jnp.float32)

@jax.custom_vjp
def low_back(v):
    return v

def low_keep(v):
    return (low(v), None)

def low_pass(kept, grad):
    return (grad,)

def back_keep(v):
    return (v, None)

def back_low(kept, grad):
    return (low(grad),)
low.defvjp(low_keep, low_pass)
low_back.defvjp(back_keep, back_low)

def layer_norm(values, gain, shift):
    center = values - lax.optimization_barrier(jnp.mean(values, axis=-1, keepdims=True))
    spread = lax.optimization_barrier(jnp.mean(center * center, axis=-1, keepdims=True))
    return center * lax.rsqrt(spread + 1e-06) * gain + shift

def layer_row(row_in, segment, valid, layer_params):
    ln1_gain, ln1_bias, query_weight, query_bias, key_weight, value_weight, value_bias, out_weight, out_bias, ln2_gain, ln2_bias, up_weight, up_bias, down_weight, down_bias = layer_params
    seq_len = row_in.shape[0]
    normed = low(layer_norm(row_in, ln1_gain, ln1_bias))
    queries = low_back(low(jnp.dot(normed, query_weight, precision=highest_mode) + query_bias))
    keys_all = low_back(low(jnp.dot(normed, key_weight, precision=highest_mode)))
    values_all = low_back(low(jnp.dot(normed, value_weight, precision=highest_mode) + value_bias))
    query_heads = queries.reshape(seq_len, HEADS, HEAD_DIM)
    key_heads = keys_all.reshape(seq_len, HEADS, HEAD_DIM)
    value_heads = values_all.reshape(seq_len, HEADS, HEAD_DIM)
    scores = jnp.einsum('qhe,khe->hqk', query_heads, key_heads, precision=highest_mode) * HEAD_DIM ** (-0.5)
    scores = low_back(scores)
    same_pic = segment[:, None] == segment[None, :]
    scores = jnp.where(same_pic[None], scores, -1e+30)
    scores = scores - lax.optimization_barrier(jnp.max(scores, axis=-1, keepdims=True))
    weights = jnp.exp(scores)
    weights = weights / lax.optimization_barrier(jnp.sum(weights, axis=-1, keepdims=True))
    weights = low(weights)
    attended = jnp.einsum('hqk,khe->qhe', weights, value_heads, precision=highest_mode)
    attended = attended.reshape(seq_len, HEADS * HEAD_DIM) * valid[:, None]
    attended = low_back(low(attended))
    branch = low_back(jnp.einsum('sc,dc->sd', attended, out_weight, precision=highest_mode) + out_bias)
    middle = row_in + branch
    normed_two = low(layer_norm(middle, ln2_gain, ln2_bias))
    hidden = low_back(jnp.dot(normed_two, up_weight, precision=highest_mode) + up_bias)
    active = low(jax.nn.gelu(hidden, approximate=True))
    mixed = low_back(jnp.einsum('sf,df->sd', active, down_weight, precision=highest_mode) + down_bias)
    return (middle + mixed) * valid[:, None]

def forward(inputs, params, segment, valid):
    current = inputs
    for layer_idx in range(LAYERS):
        layer_params = tuple((param[layer_idx] for param in params))
        row_step = jax.checkpoint(partial(layer_row, layer_params=layer_params))

        def per_row(row_items):
            return row_step(row_items[0], row_items[1], row_items[2])
        current = lax.map(per_row, (current, segment, valid))
    return current

def reference(activations, lengths, cotangent, ln1_gain, ln1_bias, query_weight, query_bias, key_weight, value_weight, value_bias, out_weight, out_bias, ln2_gain, ln2_bias, up_weight, up_bias, down_weight, down_bias):
    positions = jnp.arange(SLOTS, dtype=jnp.int32)
    ends = jnp.cumsum(lengths, axis=1).astype(jnp.int32)
    segment = lax.optimization_barrier(jnp.sum((positions[None, :, None] >= ends[:, None, :]).astype(jnp.int32), axis=2)).astype(jnp.int32)
    valid = (segment < PICS).astype(jnp.float32)
    params = tuple((weight_in.astype(jnp.float32) for weight_in in (ln1_gain, ln1_bias, query_weight, query_bias, key_weight, value_weight, value_bias, out_weight, out_bias, ln2_gain, ln2_bias, up_weight, up_bias, down_weight, down_bias)))
    inputs = activations.astype(jnp.float32)

    def run(inputs_in, params_in):
        return forward(inputs_in, params_in, segment, valid)
    output, pullback = jax.vjp(run, inputs, params)
    input_grad, grads = pullback(cotangent.astype(jnp.float32))
    return (output.astype(jnp.bfloat16), input_grad, grads[0], grads[1], grads[2], grads[3], grads[4], grads[5], grads[6], grads[7], grads[8], grads[9], grads[10], grads[11], grads[12], grads[13], grads[14])
```

```python
import functools
import math

import jax
import jax.numpy as jnp
from jax import lax
from jax.experimental import pallas as pl
from jax.experimental.pallas import tpu as pltpu
from jax.sharding import PartitionSpec as P

HEAD_DIM = 72
AUG = 8
PIC_MAX = 1024
MASKED = -1e30
BF = jnp.bfloat16
F32 = jnp.float32


def xhat_of(values):
    center = values - jnp.mean(values, axis=-1, keepdims=True)
    rstd = lax.rsqrt(jnp.mean(center * center, axis=-1, keepdims=True) + 1e-06)
    return center * rstd, rstd


def norm_back(dy, xhat, rstd, gain):
    dxhat = dy * gain
    grad = dxhat - jnp.mean(dxhat, axis=-1, keepdims=True)
    grad = (grad - xhat * jnp.mean(dxhat * xhat, axis=-1, keepdims=True)) * rstd
    return grad, jnp.sum(dy * xhat, axis=0), jnp.sum(dy, axis=0)


def gelu_tanh(values):
    return jax.nn.gelu(values, approximate=True)


def product(form, left, right):
    return jnp.einsum(form, left, right, preferred_element_type=F32)


def split3(values):
    high = lax.reduce_precision(values, 8, 7)
    rest = values - high
    mid = lax.reduce_precision(rest, 8, 7)
    return jnp.stack([high, mid, rest - mid], axis=0)


def ring_gather(piece, count):
    ring = [(i, (i + 1) % count) for i in range(count)]
    slots = [piece]
    for _ in range(count - 1):
        slots.append(lax.ppermute(slots[-1], "tp", ring))
    return slots


def ring_reduce(slots):
    count = len(slots)
    ring = [(i, (i - 1) % count) for i in range(count)]
    total = slots[-1].astype(BF)
    for s in reversed(range(count - 1)):
        total = lax.ppermute(total, "tp", ring)
        total = total.astype(F32) + slots[s].astype(F32)
        if s:
            total = total.astype(BF)
    return total


def attend_kernel(count_ref, index_ref, q_ref, k_ref, v_ref, valid_ref, o_ref, lse_ref, *, q_block, k_block):
    heads, rows, q_len = q_ref.shape
    chunks = k_ref.shape[2] // k_block
    dim = rows - AUG
    for b in range(q_len // q_block):
        cols = slice(b * q_block, (b + 1) * q_block)
        q_parts = [q_ref[h, :, cols] for h in range(heads)]

        def step(t, carry):
            start = pl.multiple_of(index_ref[b * chunks + t] * k_block, k_block)
            out = []
            for h in range(heads):
                top, acc = carry[h]
                k_part = k_ref[h, :, pl.ds(start, k_block)]
                scores = lax.dot_general(
                    k_part, q_parts[h], (((0,), (0,)), ((), ())), preferred_element_type=F32
                )
                higher = jnp.maximum(top, jnp.max(scores, axis=0, keepdims=True))
                weights = jnp.exp2(scores - higher).astype(BF)
                v_part = v_ref[h, :, pl.ds(start, k_block)]
                acc = acc * jnp.exp2(top - higher) + jnp.dot(
                    v_part, weights, preferred_element_type=F32
                )
                out.append((higher, acc))
            return tuple(out)

        first = tuple(
            (jnp.full((1, q_block), MASKED, F32), jnp.zeros((rows, q_block), F32))
            for _ in range(heads)
        )
        final = lax.fori_loop(0, count_ref[b], step, first)
        live = valid_ref[:, cols] > 0
        for h in range(heads):
            top, acc = final[h]
            total = jnp.where(live, acc[dim : dim + 1], 1.0)
            o_ref[h, :, cols] = jnp.where(live, acc[:dim] / total, 0.0).astype(BF)
            lse_ref[h, :, cols] = jnp.where(live, top + jnp.log2(total), 0.0)


def attend(q_aug, k_aug, v_aug, valid, counts, indices, q_block, k_block, group):
    heads, rows, q_len = q_aug.shape
    k_len = k_aug.shape[2]
    dim = rows - AUG
    spec = lambda r, n: pl.BlockSpec((group, r, n), lambda g, *_: (g, 0, 0))
    return pl.pallas_call(
        functools.partial(attend_kernel, q_block=q_block, k_block=k_block),
        grid_spec=pltpu.PrefetchScalarGridSpec(
            num_scalar_prefetch=2,
            grid=(heads // group,),
            in_specs=[
                spec(rows, q_len),
                spec(rows, k_len),
                spec(rows, k_len),
                pl.BlockSpec((1, q_len), lambda g, *_: (0, 0)),
            ],
            out_specs=[spec(dim, q_len), spec(1, q_len)],
        ),
        out_shape=[
            jax.ShapeDtypeStruct((heads, dim, q_len), BF),
            jax.ShapeDtypeStruct((heads, 1, q_len), F32),
        ],
        compiler_params=pltpu.CompilerParams(vmem_limit_bytes=40 << 20),
        cost_estimate=pl.CostEstimate(
            flops=4 * heads * rows * q_len * k_len,
            bytes_accessed=4 * heads * rows * (q_len + k_len),
            transcendentals=heads * q_len * k_len // 2,
        ),
        name="attend",
    )(counts, indices, q_aug, k_aug, v_aug, valid)


def attend_back_kernel(
    count_ref, index_ref, q_ref, k_ref, v_ref, g_ref, dq_ref, dk_ref, dv_ref, dk_acc, dv_acc, *, q_block, k_block
):
    heads, rows, q_len = q_ref.shape
    chunks = k_ref.shape[2] // k_block
    dim = rows - AUG
    dk_acc[...] = jnp.zeros_like(dk_acc)
    dv_acc[...] = jnp.zeros_like(dv_acc)
    for b in range(q_len // q_block):
        cols = slice(b * q_block, (b + 1) * q_block)
        q_parts = [q_ref[h, :, cols] for h in range(heads)]
        g_parts = [g_ref[h, :, cols] for h in range(heads)]

        def step(t, carry):
            start = pl.multiple_of(index_ref[b * chunks + t] * k_block, k_block)
            here = pl.ds(start, k_block)
            out = []
            for h in range(heads):
                k_part = k_ref[h, :, here]
                scores = lax.dot_general(
                    k_part, q_parts[h], (((0,), (0,)), ((), ())), preferred_element_type=F32
                )
                probs = jnp.exp2(scores)
                dprobs = lax.dot_general(
                    v_ref[h, :, here],
                    g_parts[h],
                    (((0,), (0,)), ((), ())),
                    preferred_element_type=F32,
                )
                dscores = (probs * dprobs).astype(BF)
                out.append(carry[h] + jnp.dot(k_part, dscores, preferred_element_type=F32))
                dk_acc[h, :, here] += lax.dot_general(
                    q_parts[h], dscores, (((1,), (1,)), ((), ())), preferred_element_type=F32
                )
                dv_acc[h, :, here] += lax.dot_general(
                    g_parts[h],
                    probs.astype(BF),
                    (((1,), (1,)), ((), ())),
                    preferred_element_type=F32,
                )
            return tuple(out)

        first = tuple(jnp.zeros((rows, q_block), F32) for _ in range(heads))
        final = lax.fori_loop(0, count_ref[b], step, first)
        for h in range(heads):
            dq_ref[h, :, cols] = (final[h][:dim] * dim**-0.5).astype(BF)
    for h in range(heads):
        dk_ref[h] = (dk_acc[h, :dim, :] * math.log(2.0)).astype(BF)
        dv_ref[h] = dv_acc[h, :dim, :].astype(BF)


def attend_back(q_aug, k_aug, v_aug, g_aug, counts, indices, q_block, k_block, group):
    heads, rows, q_len = q_aug.shape
    k_len = k_aug.shape[2]
    dim = rows - AUG
    spec = lambda r, n: pl.BlockSpec((group, r, n), lambda g, *_: (g, 0, 0))
    return pl.pallas_call(
        functools.partial(attend_back_kernel, q_block=q_block, k_block=k_block),
        grid_spec=pltpu.PrefetchScalarGridSpec(
            num_scalar_prefetch=2,
            grid=(heads // group,),
            in_specs=[spec(rows, q_len), spec(rows, k_len), spec(rows, k_len), spec(rows, q_len)],
            out_specs=[spec(dim, q_len), spec(dim, k_len), spec(dim, k_len)],
            scratch_shapes=[
                pltpu.VMEM((group, rows, k_len), F32),
                pltpu.VMEM((group, rows, k_len), F32),
            ],
        ),
        out_shape=[
            jax.ShapeDtypeStruct((heads, dim, q_len), BF),
            jax.ShapeDtypeStruct((heads, dim, k_len), BF),
            jax.ShapeDtypeStruct((heads, dim, k_len), BF),
        ],
        compiler_params=pltpu.CompilerParams(vmem_limit_bytes=40 << 20),
        cost_estimate=pl.CostEstimate(
            flops=10 * heads * rows * q_len * k_len,
            bytes_accessed=8 * heads * rows * (q_len + k_len),
            transcendentals=heads * q_len * k_len // 2,
        ),
        name="attend_back",
    )(counts, indices, q_aug, k_aug, v_aug, g_aug)


def local(
    activations,
    lengths,
    cotangent,
    ln1_gain,
    ln1_bias,
    query_weight,
    query_bias,
    key_weight,
    value_weight,
    value_bias,
    out_weight,
    out_bias,
    ln2_gain,
    ln2_bias,
    up_weight,
    up_bias,
    down_weight,
    down_bias,
):
    n = lax.axis_size("tp")
    me = lax.axis_index("tp")
    _, here, width = activations.shape
    total_len = here * n
    pics = lengths.shape[1]
    cols = query_weight.shape[2]
    units = up_weight.shape[2]
    heads = cols * n // HEAD_DIM
    hh = cols * n
    reach = min(n - 1, -(-(PIC_MAX - 1) // here))
    scale = HEAD_DIM**-0.5

    x_own = activations[0]
    to_left = [(i, i - 1) for i in range(1, n)]
    to_right = [(i, i + 1) for i in range(n - 1)]
    after, before = [x_own], [x_own]
    for _ in range(reach):
        after.append(lax.ppermute(after[-1], "tp", to_left))
        before.append(lax.ppermute(before[-1], "tp", to_right))
    slots = []
    token_slots = [x_own]
    for j in range(1, n):
        use_after, use_before = j <= reach, n - j <= reach
        if not (use_after or use_before):
            continue
        slots.append((j, use_after, use_before))
        if use_after and use_before:
            token_slots.append(jnp.where(me + j < n, after[j], before[n - j]))
        else:
            token_slots.append(after[j] if use_after else before[n - j])

    ends = jnp.cumsum(lengths[0])
    positions = jnp.arange(total_len, dtype=jnp.int32)
    segment = jnp.sum((positions[:, None] >= ends[None, :]).astype(jnp.int32), axis=1)
    own_seg = lax.dynamic_slice_in_dim(segment, me * here, here, 0)
    key_segs = [own_seg]
    for j, use_after, use_before in slots:
        seg = lax.dynamic_slice_in_dim(segment, ((me + j) % n) * here, here, 0)
        there = jnp.where(me + j < n, use_after, use_before)
        key_segs.append(jnp.where(there, seg, pics))
    key_seg = jnp.concatenate(key_segs)
    k_len = key_seg.shape[0]
    valid = (own_seg < pics).astype(F32)
    valid_col = valid[:, None]
    q_block = min(256, here)
    k_block = min(256, here)
    picture = jnp.arange(pics, dtype=jnp.int32)
    q_has = jnp.any(own_seg.reshape(-1, q_block, 1) == picture, axis=1)
    k_has = jnp.any(key_seg.reshape(-1, k_block, 1) == picture, axis=1)
    active = jnp.any(q_has[:, None, :] & k_has[None, :, :], axis=2)
    counts = jnp.sum(active.astype(jnp.int32), axis=1)
    place = jnp.cumsum(active.astype(jnp.int32), axis=1) - 1
    chunk_ids = jnp.arange(active.shape[1], dtype=jnp.int32)
    hit = active[:, :, None] & (place[:, :, None] == chunk_ids[None, None, :])
    indices = jnp.sum(jnp.where(hit, chunk_ids[None, :, None], 0), axis=1).reshape(-1)

    q_mask = jnp.concatenate(
        [
            jnp.where(own_seg[None, :] == picture[:, None], 0.0, MASKED),
            jnp.full((1, here), MASKED, F32),
        ],
        axis=0,
    )
    k_mask = jnp.concatenate(
        [(key_seg[None, :] == picture[:, None]), (key_seg >= pics)[None, :]], axis=0
    ).astype(BF)
    spare = AUG - (pics + 1) - 3
    k_added = jnp.concatenate(
        [k_mask, jnp.ones((3, k_len), BF), jnp.zeros((spare, k_len), BF)], axis=0
    )
    v_added = jnp.concatenate([jnp.ones((3, k_len), BF), jnp.zeros((AUG - 3, k_len), BF)], axis=0)

    def widen(body, added):
        body = body.reshape(heads, HEAD_DIM, body.shape[-1])
        added = jnp.broadcast_to(added, (heads, AUG, body.shape[-1]))
        return jnp.concatenate([body, added.astype(BF)], axis=1)

    attn_piece = jnp.concatenate(
        [query_weight[0], key_weight[0], value_weight[0], out_weight[0]], axis=1
    )
    attn_slots = ring_gather(attn_piece, n)
    vectors = jnp.stack(
        [ln1_gain[0], ln1_bias[0], out_bias[0], ln2_gain[0], ln2_bias[0], down_bias[0]], axis=1
    ).astype(BF)
    attn_shard = jnp.concatenate(
        [s[:, t * cols : (t + 1) * cols] for t in range(4) for s in attn_slots] + [vectors], axis=1
    )
    attn_full = lax.all_gather(attn_shard, "fsdp", axis=0, tiled=True)
    up_slots = ring_gather(up_weight[0], n)
    up_full = lax.all_gather(jnp.concatenate(up_slots, axis=1), "fsdp", axis=0, tiled=True)
    down_slots = ring_gather(down_weight[0], n)
    down_full = lax.all_gather(jnp.concatenate(down_slots, axis=1), "fsdp", axis=0, tiled=True)
    bias_slots = ring_gather(
        jnp.concatenate([query_bias[0], value_bias[0], up_bias[0]]), n
    )
    query_shift = jnp.concatenate([b[:cols] for b in bias_slots])
    value_shift = jnp.concatenate([b[cols : 2 * cols] for b in bias_slots])
    up_shift = jnp.concatenate([b[2 * cols :] for b in bias_slots])

    query_full = attn_full[:, :hh]
    kv_full = attn_full[:, hh : 3 * hh]
    out_full = attn_full[:, 3 * hh : 4 * hh]
    rows = attn_full[:, 4 * hh :].astype(F32).T
    gain_one, shift_one, out_shift, gain_two, shift_two, down_shift = rows

    x = x_own.astype(F32)
    tokens = jnp.concatenate(token_slots, axis=0).astype(F32)
    all_hat, _ = xhat_of(tokens)
    normed_all = (all_hat * gain_one + shift_one).astype(BF)
    normed = normed_all[:here]
    queries = (
        (product("td,dc->ct", normed, query_full) + query_shift[:, None])
        * (scale * math.log2(math.e))
    ).astype(BF)
    kv_shift = jnp.concatenate([jnp.zeros((hh,), F32), value_shift])
    keys_values = (product("td,dc->ct", normed_all, kv_full) + kv_shift[:, None]).astype(BF)
    k_aug = widen(keys_values[:hh], k_added)
    v_aug = widen(keys_values[hh:], v_added)
    q_rest = jnp.zeros((AUG - (pics + 1), here), F32)
    q_aug = widen(queries, jnp.concatenate([q_mask, q_rest], axis=0))
    group = 4 if heads % 4 == 0 else 1
    attended, log_total = attend(
        q_aug, k_aug, v_aug, valid[None, :], counts, indices, q_block, k_block, group
    )
    flat = attended.reshape(hh, here)
    middle = x + (product("ct,dc->td", flat, out_full) + out_shift)

    two_hat, two_rstd = xhat_of(middle)
    normed_two = (two_hat * gain_two + shift_two).astype(BF)
    hidden = product("td,df->tf", normed_two, up_full) + up_shift
    active_units, gelu_pull = jax.vjp(gelu_tanh, hidden)
    active_units = active_units.astype(BF)
    mixed = product("tf,df->td", active_units, down_full) + down_shift
    activations_out = ((middle + mixed) * valid_col).astype(BF)

    grad_two = cotangent[0].astype(F32) * valid_col
    grad_mixed = grad_two.astype(BF)
    down_bias_part = jnp.sum(grad_mixed, axis=0, dtype=F32)
    down_grad = product("td,tf->df", grad_mixed, active_units).astype(BF)
    down_scattered = lax.psum_scatter(down_grad, "fsdp", scatter_dimension=0, tiled=True)
    grad_hidden = gelu_pull(product("td,df->tf", grad_mixed, down_full))[0].astype(BF)
    up_bias_part = jnp.sum(grad_hidden, axis=0, dtype=F32)
    up_grad = product("td,tf->df", normed_two, grad_hidden).astype(BF)
    grad_normed_two = product("tf,df->td", grad_hidden, up_full)
    grad_middle, gain_two_part, shift_two_part = norm_back(
        grad_normed_two, two_hat, two_rstd, gain_two
    )
    grad_middle = grad_two + grad_middle
    grad_branch = grad_middle.astype(BF)
    out_bias_part = jnp.sum(grad_branch, axis=0, dtype=F32)
    out_grad = product("td,ct->dc", grad_branch, flat).astype(BF)
    early = jnp.stack([out_bias_part, gain_two_part, shift_two_part, down_bias_part], axis=1)
    up_scattered = lax.psum_scatter(
        jnp.concatenate([up_grad, out_grad, early.astype(BF)], axis=1),
        "fsdp",
        scatter_dimension=0,
        tiled=True,
    )

    grad_attended = product("td,dc->ct", grad_branch, out_full).astype(BF)
    grad_attended = grad_attended * valid.astype(BF)
    grad_heads = grad_attended.reshape(heads, HEAD_DIM, here)
    delta = jnp.sum(grad_heads.astype(F32) * attended.astype(F32), axis=1)
    g_added = jnp.concatenate(
        [
            jnp.moveaxis(split3(-delta), 0, 1),
            jnp.zeros((heads, AUG - 3, here), F32),
        ],
        axis=1,
    )
    g_aug = widen(grad_attended, g_added)
    q_added = jnp.concatenate(
        [
            jnp.broadcast_to(q_mask, (heads, pics + 1, here)),
            jnp.moveaxis(split3(-log_total[:, 0]), 0, 1),
            jnp.zeros((heads, spare, here), F32),
        ],
        axis=1,
    )
    q_aug_back = widen(queries, q_added)
    dq, dk, dv = attend_back(
        q_aug_back, k_aug, v_aug, g_aug, counts, indices, q_block, k_block, group
    )
    dq = dq.reshape(hh, here)
    dkv = jnp.concatenate([dk.reshape(hh, k_len), dv.reshape(hh, k_len)], axis=0)
    query_grad = product("td,ct->dc", normed, dq).astype(BF)
    kv_grad = product("td,ct->dc", normed_all, dkv).astype(BF)
    qkv_scattered = lax.psum_scatter(
        jnp.concatenate([query_grad, kv_grad], axis=1), "fsdp", scatter_dimension=0, tiled=True
    )
    query_bias_part = jnp.sum(dq, axis=1, dtype=F32)
    value_bias_part = jnp.sum(dv.reshape(hh, k_len), axis=1, dtype=F32)

    grad_slots = product("ct,dc->td", dkv, kv_full)
    own_share = grad_slots[:here] + product("ct,dc->td", dq, query_full)
    to_after = [None] * (reach + 1)
    to_before = [None] * (reach + 1)
    for position, (j, use_after, use_before) in enumerate(slots):
        share = grad_slots[(position + 1) * here : (position + 2) * here].astype(BF)
        zero = jnp.zeros_like(share)
        if use_after:
            to_after[j] = jnp.where(me + j < n, share, zero)
        if use_before:
            to_before[n - j] = jnp.where(me + j >= n, share, zero)
    moving_right = to_after[reach]
    moving_left = to_before[reach]
    for distance in reversed(range(1, reach + 1)):
        moving_right = lax.ppermute(moving_right, "tp", to_right).astype(F32)
        moving_left = lax.ppermute(moving_left, "tp", to_left).astype(F32)
        if distance > 1:
            moving_right = (moving_right + to_after[distance - 1].astype(F32)).astype(BF)
            moving_left = (moving_left + to_before[distance - 1].astype(F32)).astype(BF)
    grad_normed = own_share + moving_right + moving_left
    one_hat, one_rstd = xhat_of(x)
    grad_x, gain_one_part, shift_one_part = norm_back(grad_normed, one_hat, one_rstd, gain_one)
    input_grad = grad_middle + grad_x

    def owned(scattered, start, size):
        return ring_reduce(
            [scattered[:, start + s * size : start + (s + 1) * size] for s in range(n)]
        )

    down_weight_grad = owned(down_scattered, 0, units)
    up_slots_grad = [
        jnp.concatenate(
            [
                up_scattered[:, s * units : (s + 1) * units],
                up_scattered[:, n * units + s * cols : n * units + (s + 1) * cols],
            ],
            axis=1,
        )
        for s in range(n)
    ]
    up_out = ring_reduce(up_slots_grad)
    up_weight_grad, out_weight_grad = up_out[:, :units], up_out[:, units:]
    qkv_slots_grad = [
        jnp.concatenate(
            [
                qkv_scattered[:, t * hh + s * cols : t * hh + (s + 1) * cols]
                for t in range(3)
            ],
            axis=1,
        )
        for s in range(n)
    ]
    qkv_out = ring_reduce(qkv_slots_grad)
    early_sums = sum(
        s.astype(F32) for s in ring_gather(up_scattered[:, n * units + hh :].astype(F32), n)
    )

    vector_part = jnp.concatenate([gain_one_part, shift_one_part])
    bias_parts = [
        jnp.concatenate(
            [
                query_bias_part[s * cols : (s + 1) * cols],
                value_bias_part[s * cols : (s + 1) * cols],
                up_bias_part[s * units : (s + 1) * units],
            ]
        )
        for s in range(n)
    ]
    ring = [(i, (i - 1) % n) for i in range(n)]
    carried, vector_sum, passing = bias_parts[-1], vector_part, vector_part
    for s in reversed(range(n - 1)):
        moved = lax.ppermute(jnp.concatenate([carried, passing]), "tp", ring)
        carried = moved[: carried.shape[0]] + bias_parts[s]
        passing = moved[carried.shape[0] :]
        vector_sum = vector_sum + passing
    small = lax.psum(jnp.concatenate([carried, vector_sum]), "fsdp")
    bias_size = carried.shape[0]
    share = width // lax.axis_size("fsdp")
    f = lax.axis_index("fsdp")
    ln1_gain_grad = lax.dynamic_slice_in_dim(small, bias_size + f * share, share, 0)
    ln1_bias_grad = lax.dynamic_slice_in_dim(small, bias_size + width + f * share, share, 0)
    return (
        activations_out[None],
        input_grad[None],
        ln1_gain_grad[None],
        ln1_bias_grad[None],
        qkv_out[None, :, :cols],
        small[None, :cols],
        qkv_out[None, :, cols : 2 * cols],
        qkv_out[None, :, 2 * cols :],
        small[None, cols : 2 * cols],
        out_weight_grad[None],
        early_sums[None, :, 0],
        early_sums[None, :, 1],
        early_sums[None, :, 2],
        up_weight_grad[None],
        small[None, 2 * cols : bias_size],
        down_weight_grad[None],
        early_sums[None, :, 3],
    )


def solution(mesh):
    token = P("fsdp", "tp", None)
    vector, shift, matrix = P(None, "fsdp"), P(None, "tp"), P(None, "fsdp", "tp")
    in_specs = (
        token,
        P("fsdp", None),
        token,
        vector,
        vector,
        matrix,
        shift,
        matrix,
        matrix,
        shift,
        matrix,
        vector,
        vector,
        vector,
        matrix,
        shift,
        matrix,
        vector,
    )
    out_specs = (
        token,
        token,
        vector,
        vector,
        matrix,
        shift,
        matrix,
        matrix,
        shift,
        matrix,
        vector,
        vector,
        vector,
        matrix,
        shift,
        matrix,
        vector,
    )
    return jax.shard_map(local, mesh=mesh, in_specs=in_specs, out_specs=out_specs, check_vma=False)
```

```python
import functools
import math

import jax
import jax.numpy as jnp
from jax import lax
from jax.experimental import pallas as pl
from jax.experimental.pallas import tpu as pltpu
from jax.sharding import PartitionSpec as P

HEAD_DIM = 72
AUG = 8
PIC_MAX = 1024
MASKED = -1e30
BF = jnp.bfloat16
F32 = jnp.float32


def xhat_of(values):
    center = values - jnp.mean(values, axis=-1, keepdims=True)
    rstd = lax.rsqrt(jnp.mean(center * center, axis=-1, keepdims=True) + 1e-06)
    return center * rstd, rstd


def norm_back(dy, xhat, rstd, gain):
    dxhat = dy * gain
    grad = dxhat - jnp.mean(dxhat, axis=-1, keepdims=True)
    grad = (grad - xhat * jnp.mean(dxhat * xhat, axis=-1, keepdims=True)) * rstd
    return grad, jnp.sum(dy * xhat, axis=0), jnp.sum(dy, axis=0)


def gelu_tanh(values):
    return jax.nn.gelu(values, approximate=True)


def product(form, left, right):
    return jnp.einsum(form, left, right, preferred_element_type=F32)


def split3(values):
    high = lax.reduce_precision(values, 8, 7)
    rest = values - high
    mid = lax.reduce_precision(rest, 8, 7)
    return jnp.stack([high, mid, rest - mid], axis=0)


def after(value, *earlier):
    def kernel(*refs):
        pass

    return pl.pallas_call(
        kernel,
        in_specs=[pl.BlockSpec(memory_space=pl.ANY)] * (1 + len(earlier)),
        out_specs=pl.BlockSpec(memory_space=pl.ANY),
        out_shape=jax.ShapeDtypeStruct(value.shape, value.dtype),
        input_output_aliases={0: 0},
        name="after",
    )(value, *earlier)


def copy_after(value, *earlier):
    def kernel(value_ref, *refs):
        refs[-1][...] = value_ref[...]

    vmem = pl.BlockSpec(memory_space=pltpu.VMEM)
    return pl.pallas_call(
        kernel,
        in_specs=[vmem] + [pl.BlockSpec(memory_space=pl.ANY)] * len(earlier),
        out_specs=vmem,
        out_shape=jax.ShapeDtypeStruct(value.shape, value.dtype),
        name="copy_after",
    )(value, *earlier)


def slots_along_tp(piece, count, *earlier):
    slots = [piece]
    for distance in range(1, count):
        moved = lax.ppermute(piece, "tp", [(i, (i + distance) % count) for i in range(count)])
        slots.append(after(moved, *earlier) if earlier else moved)
    return slots


def by_owner(value, owners, kinds):
    rows, columns = value.shape
    size = columns // (owners * kinds)

    def kernel(value_ref, out_ref):
        for o in range(owners):
            pieces = [
                value_ref[:, (t * owners + o) * size : (t * owners + o + 1) * size]
                for t in range(kinds)
            ]
            out_ref[o] = jnp.concatenate(pieces, axis=1)

    vmem = pl.BlockSpec(memory_space=pltpu.VMEM)
    return pl.pallas_call(
        kernel,
        in_specs=[vmem],
        out_specs=vmem,
        out_shape=jax.ShapeDtypeStruct((owners, rows, kinds * size), value.dtype),
        name="by_owner",
    )(value).reshape(owners * rows, kinds * size)


def norm_kernel(*refs):
    x_refs, gain_ref, shift_ref, out_ref = refs[:-3], refs[-3], refs[-2], refs[-1]
    here, width = x_refs[0].shape
    block = math.gcd(here, 64)
    gain, shift = gain_ref[...], shift_ref[...]
    for position, x_ref in enumerate(x_refs):

        def step(i, carry):
            start = pl.multiple_of(i * block, block)
            values = x_ref[pl.ds(start, block), :].astype(F32)
            center = values - jnp.mean(values, axis=1, keepdims=True)
            spread = jnp.mean(center * center, axis=1, keepdims=True)
            result = center * lax.rsqrt(spread + 1e-06) * gain + shift
            target = pl.multiple_of(position * here + i * block, block)
            out_ref[pl.ds(target, block), :] = result.astype(BF)
            return carry

        lax.fori_loop(0, here // block, step, 0)


def norm_tokens(tokens, gain, shift):
    here, width = tokens[0].shape
    rows = here * len(tokens)
    vmem = pl.BlockSpec(memory_space=pltpu.VMEM)
    return pl.pallas_call(
        norm_kernel,
        in_specs=[vmem] * (len(tokens) + 2),
        out_specs=vmem,
        out_shape=jax.ShapeDtypeStruct((rows, width), BF),
        compiler_params=pltpu.CompilerParams(vmem_limit_bytes=32 << 20),
        cost_estimate=pl.CostEstimate(
            flops=10 * rows * width, bytes_accessed=4 * rows * width, transcendentals=rows
        ),
        name="norm_tokens",
    )(*tokens, gain[None], shift[None])


def attend_kernel(
    count_ref, index_ref, q_ref, k_ref, v_ref, valid_ref, *rest, q_block, k_block, pair
):
    o_ref, lse_ref = rest[-2:]
    heads, rows, q_len = q_ref.shape
    chunks = k_ref.shape[2] // k_block
    dim = rows - AUG
    blocks = q_len // q_block
    jobs = [(b, h) for b in range(blocks) for h in range(heads)]

    def step(t, carry):
        out = []
        for (b, h), (top, acc) in zip(jobs, carry):
            q_part = q_ref[h, :, b * q_block : (b + 1) * q_block]
            starts = [index_ref[b * chunks + t * pair + u] * k_block for u in range(pair)]
            heres = [pl.ds(pl.multiple_of(start, k_block), k_block) for start in starts]
            k_part = jnp.concatenate([k_ref[h, :, here] for here in heres], axis=1)
            v_part = jnp.concatenate([v_ref[h, :, here] for here in heres], axis=1)
            scores = lax.dot_general(
                k_part, q_part, (((0,), (0,)), ((), ())), preferred_element_type=F32
            )
            higher = jnp.maximum(top, jnp.max(scores, axis=0, keepdims=True))
            weights = jnp.exp2(scores - higher).astype(BF)
            acc = acc * jnp.exp2(top - higher) + jnp.dot(
                v_part, weights, preferred_element_type=F32
            )
            out.append((higher, acc))
        return tuple(out)

    first = tuple(
        (jnp.full((1, q_block), MASKED, F32), jnp.zeros((rows, q_block), F32)) for _ in jobs
    )
    final = lax.fori_loop(0, count_ref[0], step, first)
    for (b, h), (top, acc) in zip(jobs, final):
        cols = slice(b * q_block, (b + 1) * q_block)
        live = valid_ref[:, cols] > 0
        total = jnp.where(live, acc[dim : dim + 1], 1.0)
        o_ref[h, :, cols] = jnp.where(live, acc[:dim] / total, 0.0).astype(BF)
        lse_ref[h, :, cols] = jnp.where(live, top + jnp.log2(total), 0.0)


def attend(
    q_aug, k_aug, v_aug, valid, counts, indices, q_block, k_block, pair, group, part, parts, *earlier
):
    heads, rows, q_len = q_aug.shape
    heads = heads // parts
    base = part * (heads // group)
    k_len = k_aug.shape[2]
    dim = rows - AUG
    spec = lambda r, n: pl.BlockSpec((group, r, n), lambda g, *_: (g + base, 0, 0))
    out = lambda r, n: pl.BlockSpec((group, r, n), lambda g, *_: (g, 0, 0))
    return pl.pallas_call(
        functools.partial(attend_kernel, q_block=q_block, k_block=k_block, pair=pair),
        grid_spec=pltpu.PrefetchScalarGridSpec(
            num_scalar_prefetch=2,
            grid=(heads // group,),
            in_specs=[
                spec(rows, q_len),
                spec(rows, k_len),
                spec(rows, k_len),
                pl.BlockSpec((1, q_len), lambda g, *_: (0, 0)),
            ]
            + [pl.BlockSpec(memory_space=pl.ANY)] * len(earlier),
            out_specs=[out(dim, q_len), out(1, q_len)],
        ),
        out_shape=[
            jax.ShapeDtypeStruct((heads, dim, q_len), BF),
            jax.ShapeDtypeStruct((heads, 1, q_len), F32),
        ],
        compiler_params=pltpu.CompilerParams(vmem_limit_bytes=56 << 20),
        cost_estimate=pl.CostEstimate(
            flops=4 * heads * rows * q_len * k_len,
            bytes_accessed=4 * heads * rows * (q_len + k_len),
            transcendentals=heads * q_len * k_len // 2,
        ),
        name="attend",
    )(counts, indices, q_aug, k_aug, v_aug, valid, *earlier)


def attend_back_kernel(
    count_ref, index_ref, q_ref, k_ref, v_ref, g_ref, *rest, q_block, k_block, pair
):
    dq_ref, dkv_ref, dk_acc, dv_acc = rest[-4:]
    heads, rows, q_len = q_ref.shape
    chunks = k_ref.shape[2] // k_block
    dim = rows - AUG
    blocks = q_len // q_block
    jobs = [(b, h) for b in range(blocks) for h in range(heads)]
    dk_acc[...] = jnp.zeros_like(dk_acc)
    dv_acc[...] = jnp.zeros_like(dv_acc)

    def step(t, carry):
        out, sums = [], []
        for (b, h), dq in zip(jobs, carry):
            cols = slice(b * q_block, (b + 1) * q_block)
            q_part, g_part = q_ref[h, :, cols], g_ref[h, :, cols]
            starts = [index_ref[b * chunks + t * pair + u] * k_block for u in range(pair)]
            heres = [pl.ds(pl.multiple_of(start, k_block), k_block) for start in starts]
            k_part = jnp.concatenate([k_ref[h, :, here] for here in heres], axis=1)
            v_part = jnp.concatenate([v_ref[h, :, here] for here in heres], axis=1)
            scores = lax.dot_general(
                k_part, q_part, (((0,), (0,)), ((), ())), preferred_element_type=F32
            )
            probs = jnp.exp2(scores)
            dprobs = lax.dot_general(
                v_part, g_part, (((0,), (0,)), ((), ())), preferred_element_type=F32
            )
            dscores = (probs * dprobs).astype(BF)
            dq += jnp.dot(k_part, dscores, preferred_element_type=F32)
            dk = lax.dot_general(
                q_part, dscores, (((1,), (1,)), ((), ())), preferred_element_type=F32
            )
            dv = lax.dot_general(
                g_part, probs.astype(BF), (((1,), (1,)), ((), ())), preferred_element_type=F32
            )
            sums.append((h, heres, dk, dv))
            out.append(dq)
        for h, heres, dk, dv in sums:
            for u, here in enumerate(heres):
                dk_acc[h, :, here] += dk[:, u * k_block : (u + 1) * k_block]
                dv_acc[h, :, here] += dv[:, u * k_block : (u + 1) * k_block]
        return tuple(out)

    first = tuple(jnp.zeros((rows, q_block), F32) for _ in jobs)
    final = lax.fori_loop(0, count_ref[0], step, first)
    for (b, h), dq in zip(jobs, final):
        cols = slice(b * q_block, (b + 1) * q_block)
        dq_ref[h, :, cols] = (dq[:dim] * dim**-0.5).astype(BF)
    for h in range(heads):
        dkv_ref[0, h] = (dk_acc[h, :dim, :] * math.log(2.0)).astype(BF)
        dkv_ref[1, h] = dv_acc[h, :dim, :].astype(BF)


def attend_back(
    q_aug, k_aug, v_aug, g_aug, counts, indices, q_block, k_block, pair, group, part, parts, before, *earlier
):
    heads, rows, q_len = q_aug.shape
    k_len = k_aug.shape[2]
    dim = rows - AUG
    base = part * (heads // parts // group)
    spec = lambda r, n: pl.BlockSpec((group, r, n), lambda g, *_: (g + base, 0, 0))
    earlier = (*before, *earlier)
    return pl.pallas_call(
        functools.partial(attend_back_kernel, q_block=q_block, k_block=k_block, pair=pair),
        grid_spec=pltpu.PrefetchScalarGridSpec(
            num_scalar_prefetch=2,
            grid=(heads // parts // group,),
            in_specs=[spec(rows, q_len), spec(rows, k_len), spec(rows, k_len), spec(rows, q_len)]
            + [pl.BlockSpec(memory_space=pl.ANY)] * len(earlier),
            out_specs=[
                spec(dim, q_len),
                pl.BlockSpec((2, group, dim, k_len), lambda g, *_: (0, g + base, 0, 0)),
            ],
            scratch_shapes=[
                pltpu.VMEM((group, rows, k_len), F32),
                pltpu.VMEM((group, rows, k_len), F32),
            ],
        ),
        out_shape=[
            jax.ShapeDtypeStruct((heads, dim, q_len), BF),
            jax.ShapeDtypeStruct((2, heads, dim, k_len), BF),
        ],
        compiler_params=pltpu.CompilerParams(vmem_limit_bytes=56 << 20),
        cost_estimate=pl.CostEstimate(
            flops=10 * heads * rows * q_len * k_len,
            bytes_accessed=8 * heads * rows * (q_len + k_len),
            transcendentals=heads * q_len * k_len // 2,
        ),
        input_output_aliases={6 + i: i for i in range(len(before))},
        name="attend_back",
    )(counts, indices, q_aug, k_aug, v_aug, g_aug, *earlier)


def local(
    activations,
    lengths,
    cotangent,
    ln1_gain,
    ln1_bias,
    query_weight,
    query_bias,
    key_weight,
    value_weight,
    value_bias,
    out_weight,
    out_bias,
    ln2_gain,
    ln2_bias,
    up_weight,
    up_bias,
    down_weight,
    down_bias,
):
    n = lax.axis_size("tp")
    me = lax.axis_index("tp")
    _, here, width = activations.shape
    total_len = here * n
    pics = lengths.shape[1]
    cols = query_weight.shape[2]
    units = up_weight.shape[2]
    heads = cols * n // HEAD_DIM
    hh = cols * n
    reach = min(n - 1, -(-(PIC_MAX - 1) // here))
    scale = HEAD_DIM**-0.5

    x_own = activations[0]
    to_left = [(i, i - 1) for i in range(1, n)]
    to_right = [(i, i + 1) for i in range(n - 1)]
    ends = jnp.cumsum(lengths[0])
    positions = jnp.arange(total_len, dtype=jnp.int32)
    segment = jnp.sum((positions[:, None] >= ends[None, :]).astype(jnp.int32), axis=1)
    own_seg = lax.dynamic_slice_in_dim(segment, me * here, here, 0)
    bias_piece = jnp.concatenate([query_bias[0], value_bias[0], up_bias[0]])
    bias_terms = split3(bias_piece).astype(BF).reshape(-1)
    bias_rows = -(-bias_terms.shape[0] // (4 * cols * 8)) * 8
    bias_terms = jnp.pad(bias_terms, (0, bias_rows * 4 * cols - bias_terms.shape[0]))
    attn_piece = jnp.concatenate(
        [query_weight[0], key_weight[0], value_weight[0], out_weight[0]], axis=1
    )
    attn_piece = jnp.concatenate([attn_piece, bias_terms.reshape(bias_rows, 4 * cols)], axis=0)
    attn_parts = lax.all_gather(attn_piece, "tp", axis=0)
    vectors = jnp.concatenate([ln1_gain, ln1_bias, out_bias, ln2_gain, ln2_bias, down_bias], axis=0)
    vectors = lax.all_gather(vectors, "fsdp", axis=1, tiled=True)
    gain_one, shift_one, out_shift, gain_two, shift_two, down_shift = vectors
    slots = []
    for j in range(1, n):
        use_later, use_prior = j <= reach, n - j <= reach
        if use_later or use_prior:
            slots.append((j, use_later, use_prior))
    slots.sort(key=lambda slot: min(slot[0], n - slot[0]))
    near = 1 + sum(min(j, n - j) == 1 for j, _, _ in slots)

    key_segs = [own_seg]
    for j, use_later, use_prior in slots:
        seg = lax.dynamic_slice_in_dim(segment, ((me + j) % n) * here, here, 0)
        there = jnp.where(me + j < n, use_later, use_prior)
        key_segs.append(jnp.where(there, seg, pics))
    key_seg = jnp.concatenate(key_segs)
    k_len = key_seg.shape[0]
    valid = (own_seg < pics).astype(F32)
    valid_col = valid[:, None]
    q_block = min(512, here)
    k_block = min(256, here)
    pair = 2 if k_len % (2 * k_block) == 0 else 1
    picture = jnp.arange(pics, dtype=jnp.int32)
    q_has = jnp.any(own_seg.reshape(-1, q_block, 1) == picture, axis=1)
    k_has = jnp.any(key_seg.reshape(-1, k_block, 1) == picture, axis=1)
    active = jnp.any(q_has[:, None, :] & k_has[None, :, :], axis=2)
    used = jnp.sum(active.astype(jnp.int32), axis=1, keepdims=True)
    counts = -(-jnp.max(used, axis=0) // pair)
    place = jnp.where(
        active,
        jnp.cumsum(active.astype(jnp.int32), axis=1) - 1,
        used + jnp.cumsum(1 - active.astype(jnp.int32), axis=1) - 1,
    )
    chunk_ids = jnp.arange(active.shape[1], dtype=jnp.int32)
    hit = place[:, :, None] == chunk_ids[None, None, :]
    indices = jnp.sum(jnp.where(hit, chunk_ids[None, :, None], 0), axis=1).reshape(-1)

    q_mask = jnp.concatenate(
        [
            jnp.where(own_seg[None, :] == picture[:, None], 0.0, MASKED),
            jnp.full((1, here), MASKED, F32),
        ],
        axis=0,
    )
    k_mask = jnp.concatenate(
        [(key_seg[None, :] == picture[:, None]), (key_seg >= pics)[None, :]], axis=0
    ).astype(BF)
    spare = AUG - (pics + 1) - 3
    k_added = jnp.concatenate(
        [k_mask, jnp.ones((3, k_len), BF), jnp.zeros((spare, k_len), BF)], axis=0
    )
    v_added = jnp.concatenate([jnp.ones((3, k_len), BF), jnp.zeros((AUG - 3, k_len), BF)], axis=0)

    grad_two = cotangent[0].astype(F32) * valid_col
    grad_mixed = grad_two.astype(BF)
    down_bias_part = jnp.sum(grad_mixed, axis=0, dtype=F32)
    attn_parts = after(
        attn_parts, vectors, counts, indices, k_added, q_mask, down_bias_part, grad_mixed
    )
    share = query_weight.shape[1]
    all_biases = jnp.sum(
        attn_parts[:, share:]
        .reshape(n, -1)[:, : 3 * bias_piece.shape[0]]
        .reshape(n, 3, -1)
        .astype(F32),
        axis=1,
    )
    first = copy_after(x_own, attn_parts)
    later, prior = [first], [first]
    later.append(lax.ppermute(first, "tp", to_left))
    prior.append(lax.ppermute(first, "tp", to_right))
    query_shift = all_biases[:, :cols].reshape(-1)
    value_shift = all_biases[:, cols : 2 * cols].reshape(-1)
    ring_order = (me - jnp.arange(n)) % n
    up_shift = jnp.take(all_biases[:, 2 * cols :], ring_order, axis=0).reshape(-1)

    first_up = copy_after(
        up_weight[0], later[1], prior[1], up_shift, query_shift, value_shift
    )
    up_slots = slots_along_tp(first_up, n)
    far_later, far_prior = [later[1]], [prior[1]]
    if reach > 1:
        far_later = [after(later[1], up_slots[-1])]
        far_prior = [after(prior[1], up_slots[-1])]
    for _ in range(reach - 1):
        far_later.append(lax.ppermute(far_later[-1], "tp", to_left))
        far_prior.append(lax.ppermute(far_prior[-1], "tp", to_right))
    later, prior = [x_own] + far_later, [x_own] + far_prior

    def tokens_of(slot, *gates):
        j, use_later, use_prior = slot
        from_later = after(later[j], *gates) if use_later and gates else later[j] if use_later else None
        from_prior = after(prior[n - j], *gates) if use_prior and gates else prior[n - j] if use_prior else None
        if use_later and use_prior:
            return jnp.where(me + j < n, from_later, from_prior)
        return from_later if use_later else from_prior

    def widen(parts, added):
        parts = [part.reshape(heads, HEAD_DIM, part.shape[-1]) for part in parts]
        body = jnp.concatenate(parts, axis=2) if len(parts) > 1 else parts[0]
        added = jnp.broadcast_to(added, (heads, AUG, body.shape[-1]))
        return jnp.concatenate([body, added.astype(BF)], axis=1)

    attn_shard = jnp.concatenate(
        [attn_parts[o, :share, t * cols : (t + 1) * cols] for t in range(4) for o in range(n)],
        axis=1,
    )
    attn_full = lax.all_gather(attn_shard, "fsdp", axis=0, tiled=True)
    up_full = lax.all_gather(jnp.concatenate(up_slots, axis=1), "fsdp", axis=0, tiled=True)

    query_full = attn_full[:, :hh]
    key_full = attn_full[:, hh : 2 * hh]
    value_full = attn_full[:, 2 * hh : 3 * hh]
    kv_full = attn_full[:, hh : 3 * hh]
    out_full = attn_full[:, 3 * hh : 4 * hh]

    x = x_own.astype(F32)
    normed_near = norm_tokens(
        [x_own] + [tokens_of(slot) for slot in slots[: near - 1]], gain_one, shift_one
    )
    normed = normed_near[:here]
    queries = (
        (product("td,dc->ct", normed, query_full) + query_shift[:, None])
        * (scale * math.log2(math.e))
    ).astype(BF)
    q_rest = jnp.zeros((AUG - (pics + 1), here), F32)
    q_aug = widen([queries], jnp.concatenate([q_mask, q_rest], axis=0))

    def keys_values(tokens):
        keys = product("td,dc->ct", tokens, key_full).astype(BF)
        values = product("td,dc->ct", tokens, value_full) + value_shift[:, None]
        return keys, values.astype(BF)

    pieces = [keys_values(normed_near)]
    gates = (pieces[0][0], pieces[0][1], q_aug)
    down_first = far_later[-1], far_prior[-1]
    if slots[near - 1 :]:
        far_tokens = [tokens_of(slot, *gates) for slot in slots[near - 1 :]]
        normed_far = norm_tokens(far_tokens, gain_one, shift_one)
        pieces.append(keys_values(normed_far))
        down_first = far_tokens
    normed_all = jnp.concatenate([normed_near] + [normed_far] * (len(pieces) - 1), axis=0)
    k_aug = after(widen([piece[0] for piece in pieces], k_added))
    v_aug = after(widen([piece[1] for piece in pieces], v_added))
    group = 4 if heads % 8 == 0 else 1
    down_slots = slots_along_tp(copy_after(down_weight[0], *down_first), n, k_aug, v_aug)
    down_shard = jnp.concatenate(down_slots, axis=1)
    down_full = lax.all_gather(down_shard, "fsdp", axis=0, tiled=True)
    attended, log_total = attend(
        q_aug,
        k_aug,
        v_aug,
        valid[None, :],
        counts,
        indices,
        q_block,
        k_block,
        pair,
        group,
        0,
        1,
        down_shard,
    )
    flat = attended.reshape(hh, here)
    middle = x + (product("ct,dc->td", flat, out_full) + out_shift)

    two_hat, two_rstd = xhat_of(middle)
    normed_two = (two_hat * gain_two + shift_two).astype(BF)
    hidden = product("td,df->tf", normed_two, up_full) + up_shift
    active_units, gelu_pull = jax.vjp(gelu_tanh, hidden)
    active_units = active_units.astype(BF)

    down_grad = product("td,tf->df", grad_mixed, active_units).astype(BF)
    down_scattered = lax.psum_scatter(down_grad, "fsdp", scatter_dimension=0, tiled=True)
    back_mixed = after(grad_mixed, down_grad)
    grad_hidden = gelu_pull(product("td,df->tf", back_mixed, down_full))[0].astype(BF)
    up_bias_part = jnp.sum(grad_hidden, axis=0, dtype=F32)
    up_grad = product("td,tf->df", normed_two, grad_hidden).astype(BF)
    grad_normed_two = product("tf,df->td", grad_hidden, up_full)
    grad_middle, gain_two_part, shift_two_part = norm_back(
        grad_normed_two, two_hat, two_rstd, gain_two
    )
    grad_middle = grad_two + grad_middle
    grad_branch = grad_middle.astype(BF)
    out_bias_part = jnp.sum(grad_branch, axis=0, dtype=F32)
    out_grad = product("td,ct->dc", grad_branch, flat).astype(BF)
    up_scattered = lax.psum_scatter(up_grad, "fsdp", scatter_dimension=0, tiled=True)

    grad_attended = product("td,dc->ct", grad_branch, out_full).astype(BF)
    grad_attended = grad_attended * valid.astype(BF)
    grad_heads = grad_attended.reshape(heads, HEAD_DIM, here)
    delta = jnp.sum(grad_heads.astype(F32) * attended.astype(F32), axis=1)
    g_added = jnp.concatenate(
        [
            jnp.moveaxis(split3(-delta), 0, 1),
            jnp.zeros((heads, AUG - 3, here), F32),
        ],
        axis=1,
    )
    g_aug = widen([grad_attended], g_added)
    q_added = jnp.concatenate(
        [
            jnp.broadcast_to(q_mask, (heads, pics + 1, here)),
            jnp.moveaxis(split3(-log_total[:, 0]), 0, 1),
            jnp.zeros((heads, spare, here), F32),
        ],
        axis=1,
    )
    q_aug_back = widen([queries], q_added)
    def back_part(part, before, *earlier):
        return attend_back(
            q_aug_back,
            k_aug,
            v_aug,
            g_aug,
            counts,
            indices,
            q_block,
            k_block,
            pair,
            group,
            part,
            2,
            before,
            *earlier,
        )

    parts = back_part(0, (), up_grad, out_grad)
    down_scattered = after(down_scattered, parts[0])
    down_moved = [
        lax.ppermute(
            down_scattered[:, s * units : (s + 1) * units],
            "tp",
            [(i, (i - s) % n) for i in range(n)],
        )
        for s in range(1, n)
    ]
    dq, dkv = back_part(1, parts, down_scattered)
    down_moved = [after(moved, dq) for moved in down_moved]
    dq, dkv = dq.reshape(hh, -1), dkv.reshape(2 * hh, -1)

    def share_of(position, dkv):
        part = slice(position * here, (position + 1) * here)
        return product("ct,dc->td", dkv[:, part], kv_full)

    to_later = [None] * (reach + 1)
    to_prior = [None] * (reach + 1)

    def send_shares(distance, dkv):
        for i, (j, use_later, use_prior) in enumerate(slots):
            if min(j, n - j) != distance:
                continue
            part = share_of(i + 1, dkv).astype(BF)
            zero = jnp.zeros_like(part)
            if use_later and j == distance:
                to_later[j] = jnp.where(me + j < n, part, zero)
            if use_prior and n - j == distance:
                to_prior[n - j] = jnp.where(me + j >= n, part, zero)

    send_shares(reach, dkv)
    moving_right = lax.ppermute(to_later[reach], "tp", to_right)
    moving_left = lax.ppermute(to_prior[reach], "tp", to_left)
    dkv = after(dkv, to_later[reach], to_prior[reach], *down_moved)
    query_grad = product("td,ct->dc", normed, dq).astype(BF)
    kv_grad = product("td,ct->dc", normed_all, dkv).astype(BF)
    out_grad = after(out_grad, kv_grad, query_grad, moving_right, moving_left)
    attn_grad = jnp.concatenate([query_grad, kv_grad, out_grad], axis=1)
    attn_scattered = lax.psum_scatter(attn_grad, "fsdp", scatter_dimension=0, tiled=True)
    query_bias_part = jnp.sum(dq, axis=1, dtype=F32)
    dkv = after(dkv, attn_grad)
    for distance in reversed(range(1, reach)):
        send_shares(distance, dkv)
    up_moved = [
        lax.ppermute(
            up_scattered[:, s * units : (s + 1) * units],
            "tp",
            [(i, (i - s) % n) for i in range(n)],
        )
        for s in range(1, n)
    ]
    near_shares = [t for t in to_later[1:] + to_prior[1:] if t is not None]
    for distance in reversed(range(1, reach)):
        up_moved = [after(moved, *near_shares) for moved in up_moved]
        moving_right = after(moving_right, *near_shares, *up_moved)
        moving_left = after(moving_left, *near_shares)
        moving_right = (moving_right.astype(F32) + to_later[distance].astype(F32)).astype(BF)
        moving_left = (moving_left.astype(F32) + to_prior[distance].astype(F32)).astype(BF)
        dkv = after(dkv, moving_right, moving_left)
        moving_right = lax.ppermute(moving_right, "tp", to_right)
        moving_left = lax.ppermute(moving_left, "tp", to_left)
    own_share = share_of(0, dkv) + product("ct,dc->td", dq, query_full)
    moving_right, moving_left = after(moving_right, own_share), after(moving_left, own_share)
    grad_normed = own_share + moving_right.astype(F32) + moving_left.astype(F32)

    def summed(scattered, moved):
        return sum((m.astype(F32) for m in moved), scattered[:, :units].astype(F32))

    down_weight_grad = summed(down_scattered, down_moved)
    up_weight_grad = summed(up_scattered, up_moved)
    one_hat, one_rstd = xhat_of(x)
    grad_x, gain_one_part, shift_one_part = norm_back(grad_normed, one_hat, one_rstd, gain_one)
    input_grad = grad_middle + grad_x

    value_bias_part = jnp.sum(dkv[hh:], axis=1, dtype=F32)
    vector_part = jnp.concatenate(
        [
            gain_one_part,
            shift_one_part,
            out_bias_part,
            gain_two_part,
            shift_two_part,
            down_bias_part,
        ]
    )
    up_bias_parts = jnp.take(up_bias_part.reshape(n, units), ring_order, axis=0).reshape(-1)
    small = jnp.concatenate([query_bias_part, value_bias_part, up_bias_parts, vector_part])

    def sum_over(value, axis):
        count = lax.axis_size(axis)
        if count & (count - 1):
            return lax.psum(value, axis)
        bit = 1
        while bit < count:
            value = value + lax.ppermute(value, axis, [(i, i ^ bit) for i in range(count)])
            bit *= 2
        return value

    small = sum_over(sum_over(small, "tp"), "fsdp")
    attn_scattered = after(attn_scattered, small)
    attn_owned = by_owner(attn_scattered, n, 4)
    attn_out = lax.psum_scatter(attn_owned, "tp", scatter_dimension=0, tiled=True).astype(F32)
    mixed = product("tf,df->td", after(active_units, attn_owned), down_full) + down_shift
    activations_out = ((middle + mixed) * valid_col).astype(BF)

    bias_size = (2 * cols + units) * n
    query_bias_grad, value_bias_grad, up_bias_grad = (
        lax.dynamic_slice_in_dim(small, start + me * size, size, 0)
        for start, size in ((0, cols), (hh, cols), (2 * hh, units))
    )
    own_vectors = lax.dynamic_slice_in_dim(
        small[bias_size:].reshape(6, width), lax.axis_index("fsdp") * share, share, 1
    )
    return (
        activations_out[None],
        input_grad[None],
        own_vectors[0:1],
        own_vectors[1:2],
        attn_out[None, :, :cols],
        query_bias_grad[None],
        attn_out[None, :, cols : 2 * cols],
        attn_out[None, :, 2 * cols : 3 * cols],
        value_bias_grad[None],
        attn_out[None, :, 3 * cols :],
        own_vectors[2:3],
        own_vectors[3:4],
        own_vectors[4:5],
        up_weight_grad[None],
        up_bias_grad[None],
        down_weight_grad[None],
        own_vectors[5:6],
    )


def solution(mesh):
    token = P("fsdp", "tp", None)
    vector, shift, matrix = P(None, "fsdp"), P(None, "tp"), P(None, "fsdp", "tp")
    in_specs = (
        token,
        P("fsdp", None),
        token,
        vector,
        vector,
        matrix,
        shift,
        matrix,
        matrix,
        shift,
        matrix,
        vector,
        vector,
        vector,
        matrix,
        shift,
        matrix,
        vector,
    )
    out_specs = (
        token,
        token,
        vector,
        vector,
        matrix,
        shift,
        matrix,
        matrix,
        shift,
        matrix,
        vector,
        vector,
        vector,
        matrix,
        shift,
        matrix,
        vector,
    )
    return jax.shard_map(local, mesh=mesh, in_specs=in_specs, out_specs=out_specs, check_vma=False)
```

```python
import functools
import math

import jax
import jax.numpy as jnp
from jax import lax
from jax.experimental import pallas as pl
from jax.experimental.pallas import tpu as pltpu
from jax.sharding import PartitionSpec as P

HEAD_DIM = 72
AUG = 8
PIC_MAX = 1024
MASKED = -1e30
BF = jnp.bfloat16
F32 = jnp.float32


def xhat_of(values):
    center = values - jnp.mean(values, axis=-1, keepdims=True)
    rstd = lax.rsqrt(jnp.mean(center * center, axis=-1, keepdims=True) + 1e-06)
    return center * rstd, rstd


def norm_back(dy, xhat, rstd, gain):
    dxhat = dy * gain
    grad = dxhat - jnp.mean(dxhat, axis=-1, keepdims=True)
    grad = (grad - xhat * jnp.mean(dxhat * xhat, axis=-1, keepdims=True)) * rstd
    return grad, jnp.sum(dy * xhat, axis=0), jnp.sum(dy, axis=0)


def gelu_tanh(values):
    return jax.nn.gelu(values, approximate=True)


def product(form, left, right):
    return jnp.einsum(form, left, right, preferred_element_type=F32)


def split3(values):
    high = lax.reduce_precision(values, 8, 7)
    rest = values - high
    mid = lax.reduce_precision(rest, 8, 7)
    return jnp.stack([high, mid, rest - mid], axis=0)


def after(value, *earlier):
    def kernel(*refs):
        pass

    return pl.pallas_call(
        kernel,
        in_specs=[pl.BlockSpec(memory_space=pl.ANY)] * (1 + len(earlier)),
        out_specs=pl.BlockSpec(memory_space=pl.ANY),
        out_shape=jax.ShapeDtypeStruct(value.shape, value.dtype),
        input_output_aliases={0: 0},
        compiler_params=pltpu.CompilerParams(vmem_limit_bytes=54 << 20),
        name="after",
    )(value, *earlier)


def copy_after(value, *earlier):
    def kernel(value_ref, *refs):
        refs[-1][...] = value_ref[...]

    vmem = pl.BlockSpec(memory_space=pltpu.VMEM)
    return pl.pallas_call(
        kernel,
        in_specs=[vmem] + [pl.BlockSpec(memory_space=pl.ANY)] * len(earlier),
        out_specs=vmem,
        out_shape=jax.ShapeDtypeStruct(value.shape, value.dtype),
        compiler_params=pltpu.CompilerParams(vmem_limit_bytes=54 << 20),
        name="copy_after",
    )(value, *earlier)


def slots_along_tp(piece, count, *earlier):
    slots = [piece]
    for distance in range(1, count):
        moved = lax.ppermute(piece, "tp", [(i, (i + distance) % count) for i in range(count)])
        slots.append(after(moved, *earlier) if earlier else moved)
    return slots


def by_owner(value, owners, kinds):
    rows, columns = value.shape
    size = columns // (owners * kinds)

    def kernel(value_ref, out_ref):
        for o in range(owners):
            pieces = [
                value_ref[:, (t * owners + o) * size : (t * owners + o + 1) * size]
                for t in range(kinds)
            ]
            out_ref[o] = jnp.concatenate(pieces, axis=1)

    vmem = pl.BlockSpec(memory_space=pltpu.VMEM)
    return pl.pallas_call(
        kernel,
        in_specs=[vmem],
        out_specs=vmem,
        out_shape=jax.ShapeDtypeStruct((owners, rows, kinds * size), value.dtype),
        compiler_params=pltpu.CompilerParams(vmem_limit_bytes=54 << 20),
        name="by_owner",
    )(value).reshape(owners * rows, kinds * size)


def norm_kernel(x_ref, gain_ref, shift_ref, *rest):
    values = x_ref[...].astype(F32)
    center = values - jnp.mean(values, axis=1, keepdims=True)
    spread = jnp.mean(center * center, axis=1, keepdims=True)
    result = center * lax.rsqrt(spread + 1e-06) * gain_ref[...] + shift_ref[...]
    rest[-1][...] = result.astype(BF)


def norm_slot(tokens, gain, shift, slot, slots, *into):
    here, width = tokens.shape
    block = math.gcd(here, 128)
    steps = here // block
    whole = pl.BlockSpec((1, width), lambda i: (0, 0))
    return pl.pallas_call(
        norm_kernel,
        grid=(steps,),
        in_specs=[pl.BlockSpec((block, width), lambda i: (i, 0)), whole, whole]
        + [pl.BlockSpec(memory_space=pl.ANY)] * len(into),
        out_specs=pl.BlockSpec((block, width), lambda i: (slot * steps + i, 0)),
        out_shape=jax.ShapeDtypeStruct((slots * here, width), BF),
        input_output_aliases={3: 0} if into else {},
        cost_estimate=pl.CostEstimate(
            flops=10 * here * width, bytes_accessed=4 * here * width, transcendentals=here
        ),
        compiler_params=pltpu.CompilerParams(vmem_limit_bytes=54 << 20),
        name="norm_slot",
    )(tokens, gain[None], shift[None], *into)


def attend_kernel(
    count_ref, index_ref, q_ref, k_ref, v_ref, valid_ref, *rest, q_block, k_block, pair
):
    o_ref, lse_ref = rest[-2:]
    heads, rows, q_len = q_ref.shape
    chunks = k_ref.shape[2] // k_block
    dim = rows - AUG
    blocks = q_len // q_block
    jobs = [(b, h) for b in range(blocks) for h in range(heads)]

    def step(t, carry):
        out = []
        for (b, h), (top, acc) in zip(jobs, carry):
            q_part = q_ref[h, :, b * q_block : (b + 1) * q_block]
            starts = [index_ref[b * chunks + t * pair + u] * k_block for u in range(pair)]
            heres = [pl.ds(pl.multiple_of(start, k_block), k_block) for start in starts]
            k_part = jnp.concatenate([k_ref[h, :, here] for here in heres], axis=1)
            v_part = jnp.concatenate([v_ref[h, :, here] for here in heres], axis=1)
            scores = lax.dot_general(
                k_part, q_part, (((0,), (0,)), ((), ())), preferred_element_type=F32
            )
            higher = jnp.maximum(top, jnp.max(scores, axis=0, keepdims=True))
            weights = jnp.exp2(scores - higher).astype(BF)
            acc = acc * jnp.exp2(top - higher) + jnp.dot(
                v_part, weights, preferred_element_type=F32
            )
            out.append((higher, acc))
        return tuple(out)

    first = tuple(
        (jnp.full((1, q_block), MASKED, F32), jnp.zeros((rows, q_block), F32)) for _ in jobs
    )
    final = lax.fori_loop(0, count_ref[0], step, first)
    for (b, h), (top, acc) in zip(jobs, final):
        cols = slice(b * q_block, (b + 1) * q_block)
        live = valid_ref[:, cols] > 0
        total = jnp.where(live, acc[dim : dim + 1], 1.0)
        o_ref[h, :, cols] = jnp.where(live, acc[:dim] / total, 0.0).astype(BF)
        lse_ref[h, :, cols] = jnp.where(live, top + jnp.log2(total), 0.0)


def attend(
    q_aug, k_aug, v_aug, valid, counts, indices, q_block, k_block, pair, group, part, parts, *earlier
):
    heads, rows, q_len = q_aug.shape
    heads = heads // parts
    base = part * (heads // group)
    k_len = k_aug.shape[2]
    dim = rows - AUG
    spec = lambda r, n: pl.BlockSpec((group, r, n), lambda g, *_: (g + base, 0, 0))
    out = lambda r, n: pl.BlockSpec((group, r, n), lambda g, *_: (g, 0, 0))
    return pl.pallas_call(
        functools.partial(attend_kernel, q_block=q_block, k_block=k_block, pair=pair),
        grid_spec=pltpu.PrefetchScalarGridSpec(
            num_scalar_prefetch=2,
            grid=(heads // group,),
            in_specs=[
                spec(rows, q_len),
                spec(rows, k_len),
                spec(rows, k_len),
                pl.BlockSpec((1, q_len), lambda g, *_: (0, 0)),
            ]
            + [pl.BlockSpec(memory_space=pl.ANY)] * len(earlier),
            out_specs=[out(dim, q_len), out(1, q_len)],
        ),
        out_shape=[
            jax.ShapeDtypeStruct((heads, dim, q_len), BF),
            jax.ShapeDtypeStruct((heads, 1, q_len), F32),
        ],
        compiler_params=pltpu.CompilerParams(vmem_limit_bytes=54 << 20),
        cost_estimate=pl.CostEstimate(
            flops=4 * heads * rows * q_len * k_len,
            bytes_accessed=4 * heads * rows * (q_len + k_len),
            transcendentals=heads * q_len * k_len // 2,
        ),
        name="attend",
    )(counts, indices, q_aug, k_aug, v_aug, valid, *earlier)


def attend_back_kernel(
    count_ref, index_ref, q_ref, k_ref, v_ref, g_ref, *rest, q_block, k_block, pair
):
    dq_ref, dkv_ref, dk_acc, dv_acc = rest[-4:]
    heads, rows, q_len = q_ref.shape
    chunks = k_ref.shape[2] // k_block
    dim = rows - AUG
    blocks = q_len // q_block
    jobs = [(b, h) for b in range(blocks) for h in range(heads)]
    dk_acc[...] = jnp.zeros_like(dk_acc)
    dv_acc[...] = jnp.zeros_like(dv_acc)

    def step(t, carry):
        out, sums = [], []
        for (b, h), dq in zip(jobs, carry):
            cols = slice(b * q_block, (b + 1) * q_block)
            q_part, g_part = q_ref[h, :, cols], g_ref[h, :, cols]
            starts = [index_ref[b * chunks + t * pair + u] * k_block for u in range(pair)]
            heres = [pl.ds(pl.multiple_of(start, k_block), k_block) for start in starts]
            k_part = jnp.concatenate([k_ref[h, :, here] for here in heres], axis=1)
            v_part = jnp.concatenate([v_ref[h, :, here] for here in heres], axis=1)
            scores = lax.dot_general(
                k_part, q_part, (((0,), (0,)), ((), ())), preferred_element_type=F32
            )
            probs = jnp.exp2(scores)
            dprobs = lax.dot_general(
                v_part, g_part, (((0,), (0,)), ((), ())), preferred_element_type=F32
            )
            dscores = (probs * dprobs).astype(BF)
            dq += jnp.dot(k_part, dscores, preferred_element_type=F32)
            dk = lax.dot_general(
                q_part, dscores, (((1,), (1,)), ((), ())), preferred_element_type=F32
            )
            dv = lax.dot_general(
                g_part, probs.astype(BF), (((1,), (1,)), ((), ())), preferred_element_type=F32
            )
            sums.append((h, heres, dk, dv))
            out.append(dq)
        for h, heres, dk, dv in sums:
            for u, here in enumerate(heres):
                dk_acc[h, :, here] += dk[:, u * k_block : (u + 1) * k_block]
                dv_acc[h, :, here] += dv[:, u * k_block : (u + 1) * k_block]
        return tuple(out)

    first = tuple(jnp.zeros((rows, q_block), F32) for _ in jobs)
    final = lax.fori_loop(0, count_ref[0], step, first)
    for (b, h), dq in zip(jobs, final):
        cols = slice(b * q_block, (b + 1) * q_block)
        dq_ref[h, :, cols] = (dq[:dim] * dim**-0.5).astype(BF)
    for h in range(heads):
        dkv_ref[0, h] = (dk_acc[h, :dim, :] * math.log(2.0)).astype(BF)
        dkv_ref[1, h] = dv_acc[h, :dim, :].astype(BF)


def attend_back(
    q_aug, k_aug, v_aug, g_aug, counts, indices, q_block, k_block, pair, group, part, parts, before, *earlier
):
    heads, rows, q_len = q_aug.shape
    k_len = k_aug.shape[2]
    dim = rows - AUG
    base = part * (heads // parts // group)
    spec = lambda r, n: pl.BlockSpec((group, r, n), lambda g, *_: (g + base, 0, 0))
    earlier = (*before, *earlier)
    return pl.pallas_call(
        functools.partial(attend_back_kernel, q_block=q_block, k_block=k_block, pair=pair),
        grid_spec=pltpu.PrefetchScalarGridSpec(
            num_scalar_prefetch=2,
            grid=(heads // parts // group,),
            in_specs=[spec(rows, q_len), spec(rows, k_len), spec(rows, k_len), spec(rows, q_len)]
            + [pl.BlockSpec(memory_space=pl.ANY)] * len(earlier),
            out_specs=[
                spec(dim, q_len),
                pl.BlockSpec((2, group, dim, k_len), lambda g, *_: (0, g + base, 0, 0)),
            ],
            scratch_shapes=[
                pltpu.VMEM((group, rows, k_len), F32),
                pltpu.VMEM((group, rows, k_len), F32),
            ],
        ),
        out_shape=[
            jax.ShapeDtypeStruct((heads, dim, q_len), BF),
            jax.ShapeDtypeStruct((2, heads, dim, k_len), BF),
        ],
        compiler_params=pltpu.CompilerParams(vmem_limit_bytes=54 << 20),
        cost_estimate=pl.CostEstimate(
            flops=10 * heads * rows * q_len * k_len,
            bytes_accessed=8 * heads * rows * (q_len + k_len),
            transcendentals=heads * q_len * k_len // 2,
        ),
        input_output_aliases={6 + i: i for i in range(len(before))},
        name="attend_back",
    )(counts, indices, q_aug, k_aug, v_aug, g_aug, *earlier)


def local(
    activations,
    lengths,
    cotangent,
    ln1_gain,
    ln1_bias,
    query_weight,
    query_bias,
    key_weight,
    value_weight,
    value_bias,
    out_weight,
    out_bias,
    ln2_gain,
    ln2_bias,
    up_weight,
    up_bias,
    down_weight,
    down_bias,
):
    n = lax.axis_size("tp")
    me = lax.axis_index("tp")
    _, here, width = activations.shape
    total_len = here * n
    pics = lengths.shape[1]
    cols = query_weight.shape[2]
    units = up_weight.shape[2]
    heads = cols * n // HEAD_DIM
    hh = cols * n
    reach = min(n - 1, -(-(PIC_MAX - 1) // here))
    scale = HEAD_DIM**-0.5

    x_own = activations[0]
    to_left = [(i, i - 1) for i in range(1, n)]
    to_right = [(i, i + 1) for i in range(n - 1)]
    ends = jnp.cumsum(lengths[0])
    positions = jnp.arange(total_len, dtype=jnp.int32)
    segment = jnp.sum((positions[:, None] >= ends[None, :]).astype(jnp.int32), axis=1)
    own_seg = lax.dynamic_slice_in_dim(segment, me * here, here, 0)
    bias_piece = jnp.concatenate([query_bias[0], value_bias[0], up_bias[0]])
    bias_terms = split3(bias_piece).astype(BF).reshape(-1)
    bias_rows = -(-bias_terms.shape[0] // (3 * cols * 8)) * 8
    bias_terms = jnp.pad(bias_terms, (0, bias_rows * 3 * cols - bias_terms.shape[0]))
    attn_piece = jnp.concatenate([query_weight[0], key_weight[0], value_weight[0]], axis=1)
    attn_piece = jnp.concatenate([attn_piece, bias_terms.reshape(bias_rows, 3 * cols)], axis=0)
    attn_parts = lax.all_gather(attn_piece, "tp", axis=0)
    vectors = jnp.concatenate([ln1_gain, ln1_bias, out_bias, ln2_gain, ln2_bias, down_bias], axis=0)
    vectors = lax.all_gather(vectors, "fsdp", axis=1, tiled=True)
    gain_one, shift_one, out_shift, gain_two, shift_two, down_shift = vectors
    slots = []
    for j in range(1, n):
        use_later, use_prior = j <= reach, n - j <= reach
        if use_later or use_prior:
            slots.append((j, use_later, use_prior))
    slots.sort(key=lambda slot: min(slot[0], n - slot[0]))

    key_segs = [own_seg]
    for j, use_later, use_prior in slots:
        seg = lax.dynamic_slice_in_dim(segment, ((me + j) % n) * here, here, 0)
        there = jnp.where(me + j < n, use_later, use_prior)
        key_segs.append(jnp.where(there, seg, pics))
    key_seg = jnp.concatenate(key_segs)
    k_len = key_seg.shape[0]
    valid = (own_seg < pics).astype(F32)
    valid_col = valid[:, None]
    q_block = min(512, here)
    k_block = min(256, here)
    pair = 2 if k_len % (2 * k_block) == 0 else 1
    picture = jnp.arange(pics, dtype=jnp.int32)
    q_has = jnp.any(own_seg.reshape(-1, q_block, 1) == picture, axis=1)
    k_has = jnp.any(key_seg.reshape(-1, k_block, 1) == picture, axis=1)
    active = jnp.any(q_has[:, None, :] & k_has[None, :, :], axis=2)
    used = jnp.sum(active.astype(jnp.int32), axis=1, keepdims=True)
    counts = -(-jnp.max(used, axis=0) // pair)
    place = jnp.where(
        active,
        jnp.cumsum(active.astype(jnp.int32), axis=1) - 1,
        used + jnp.cumsum(1 - active.astype(jnp.int32), axis=1) - 1,
    )
    chunk_ids = jnp.arange(active.shape[1], dtype=jnp.int32)
    hit = place[:, :, None] == chunk_ids[None, None, :]
    indices = jnp.sum(jnp.where(hit, chunk_ids[None, :, None], 0), axis=1).reshape(-1)

    q_mask = jnp.concatenate(
        [
            jnp.where(own_seg[None, :] == picture[:, None], 0.0, MASKED),
            jnp.full((1, here), MASKED, F32),
        ],
        axis=0,
    )
    k_mask = jnp.concatenate(
        [(key_seg[None, :] == picture[:, None]), (key_seg >= pics)[None, :]], axis=0
    ).astype(BF)
    spare = AUG - (pics + 1) - 3
    k_added = jnp.concatenate(
        [k_mask, jnp.ones((3, k_len), BF), jnp.zeros((spare, k_len), BF)], axis=0
    )
    v_added = jnp.concatenate([jnp.ones((3, k_len), BF), jnp.zeros((AUG - 3, k_len), BF)], axis=0)

    grad_two = cotangent[0].astype(F32) * valid_col
    grad_mixed = grad_two.astype(BF)
    down_bias_part = jnp.sum(grad_mixed, axis=0, dtype=F32)
    later = [x_own, lax.ppermute(x_own, "tp", to_left)]
    prior = [x_own, lax.ppermute(x_own, "tp", to_right)]
    attn_parts = after(
        attn_parts,
        vectors,
        counts,
        indices,
        k_added,
        q_mask,
        down_bias_part,
        grad_mixed,
        later[1],
        prior[1],
    )
    share = query_weight.shape[1]
    all_biases = jnp.sum(
        attn_parts[:, share:]
        .reshape(n, -1)[:, : 3 * bias_piece.shape[0]]
        .reshape(n, 3, -1)
        .astype(F32),
        axis=1,
    )
    query_shift = all_biases[:, :cols].reshape(-1)
    value_shift = all_biases[:, cols : 2 * cols].reshape(-1)
    ring_order = (me - jnp.arange(n)) % n
    up_shift = jnp.take(all_biases[:, 2 * cols :], ring_order, axis=0).reshape(-1)
    wide_piece = jnp.concatenate([out_weight[0], up_weight[0]], axis=1)
    wide_slots = slots_along_tp(
        copy_after(wide_piece, attn_parts, up_shift, query_shift, value_shift), n
    )
    later[1], prior[1] = after(later[1], *wide_slots[1:]), after(prior[1], *wide_slots[1:])
    for _ in range(reach - 1):
        later.append(lax.ppermute(later[-1], "tp", to_left))
        prior.append(lax.ppermute(prior[-1], "tp", to_right))

    slot_count = 1 + len(slots)
    normed_all = norm_slot(x_own, gain_one, shift_one, 0, slot_count)
    for position, (j, use_later, use_prior) in enumerate(slots):
        if use_later and use_prior:
            tokens = jnp.where(me + j < n, later[j], prior[n - j])
        else:
            tokens = later[j] if use_later else prior[n - j]
        if min(j, n - j) == 1:
            normed_all = norm_slot(
                tokens, gain_one, shift_one, position + 1, slot_count, normed_all
            )
        else:
            normed_all = norm_slot(
                tokens, gain_one, shift_one, position + 1, slot_count, normed_all
            )
    first_down = copy_after(down_weight[0], later[-1], prior[-1])

    def widen(body, added):
        body = body.reshape(heads, HEAD_DIM, body.shape[-1])
        added = jnp.broadcast_to(added, (heads, AUG, body.shape[-1]))
        return jnp.concatenate([body, added.astype(BF)], axis=1)

    attn_shard = jnp.concatenate(
        [attn_parts[o, :share, t * cols : (t + 1) * cols] for t in range(3) for o in range(n)],
        axis=1,
    )
    attn_full = lax.all_gather(attn_shard, "fsdp", axis=0, tiled=True)
    out_slots = jnp.take(jnp.stack([s[:, :cols] for s in wide_slots]), ring_order, axis=0)
    wide_shard = jnp.concatenate(
        [out_slots[o] for o in range(n)] + [s[:, cols:] for s in wide_slots], axis=1
    )
    wide_full = lax.all_gather(wide_shard, "fsdp", axis=0, tiled=True)
    out_full, up_full = wide_full[:, :hh], wide_full[:, hh:]

    query_full = attn_full[:, :hh]
    key_full = attn_full[:, hh : 2 * hh]
    value_full = attn_full[:, 2 * hh : 3 * hh]
    kv_full = attn_full[:, hh : 3 * hh]

    x = x_own.astype(F32)
    normed = normed_all[:here]
    queries = (
        (product("td,dc->ct", normed, query_full) + query_shift[:, None])
        * (scale * math.log2(math.e))
    ).astype(BF)
    q_rest = jnp.zeros((AUG - (pics + 1), here), F32)
    q_aug = widen(queries, jnp.concatenate([q_mask, q_rest], axis=0))

    keys = product("td,dc->ct", normed_all, key_full).astype(BF)
    values = product("td,dc->ct", normed_all, value_full) + value_shift[:, None]
    k_aug = after(widen(keys, k_added))
    v_aug = after(widen(values.astype(BF), v_added))
    down_slots = slots_along_tp(first_down, n, k_aug, v_aug)
    group = 4 if heads % 8 == 0 else 1
    down_shard = jnp.concatenate(down_slots, axis=1)
    down_full = lax.all_gather(down_shard, "fsdp", axis=0, tiled=True)
    attended, log_total = attend(
        q_aug,
        k_aug,
        v_aug,
        valid[None, :],
        counts,
        indices,
        q_block,
        k_block,
        pair,
        group,
        0,
        1,
        down_shard,
    )
    flat = attended.reshape(hh, here)
    middle = x + (product("ct,dc->td", flat, out_full) + out_shift)

    two_hat, two_rstd = xhat_of(middle)
    normed_two = (two_hat * gain_two + shift_two).astype(BF)
    hidden = product("td,df->tf", normed_two, up_full) + up_shift
    active_units, gelu_pull = jax.vjp(gelu_tanh, hidden)
    active_units = active_units.astype(BF)

    down_grad = product("td,tf->df", grad_mixed, active_units).astype(BF)
    down_scattered = lax.psum_scatter(down_grad, "fsdp", scatter_dimension=0, tiled=True)
    back_mixed = after(grad_mixed, down_grad)
    grad_hidden = gelu_pull(product("td,df->tf", back_mixed, down_full))[0].astype(BF)
    up_bias_part = jnp.sum(grad_hidden, axis=0, dtype=F32)
    up_grad = product("td,tf->df", normed_two, grad_hidden).astype(BF)
    grad_normed_two = product("tf,df->td", grad_hidden, up_full)
    grad_middle, gain_two_part, shift_two_part = norm_back(
        grad_normed_two, two_hat, two_rstd, gain_two
    )
    grad_middle = grad_two + grad_middle
    grad_branch = grad_middle.astype(BF)
    out_bias_part = jnp.sum(grad_branch, axis=0, dtype=F32)
    out_grad = product("td,ct->dc", grad_branch, flat).astype(BF)
    up_scattered = lax.psum_scatter(up_grad, "fsdp", scatter_dimension=0, tiled=True)

    grad_attended = product("td,dc->ct", grad_branch, out_full).astype(BF)
    grad_attended = grad_attended * valid.astype(BF)
    grad_heads = grad_attended.reshape(heads, HEAD_DIM, here)
    delta = jnp.sum(grad_heads.astype(F32) * attended.astype(F32), axis=1)
    g_added = jnp.concatenate(
        [
            jnp.moveaxis(split3(-delta), 0, 1),
            jnp.zeros((heads, AUG - 3, here), F32),
        ],
        axis=1,
    )
    g_aug = widen(grad_attended, g_added)
    q_added = jnp.concatenate(
        [
            jnp.broadcast_to(q_mask, (heads, pics + 1, here)),
            jnp.moveaxis(split3(-log_total[:, 0]), 0, 1),
            jnp.zeros((heads, spare, here), F32),
        ],
        axis=1,
    )
    q_aug_back = widen(queries, q_added)
    def back_part(part, before, *earlier):
        return attend_back(
            q_aug_back,
            k_aug,
            v_aug,
            g_aug,
            counts,
            indices,
            q_block,
            k_block,
            pair,
            group,
            part,
            2,
            before,
            *earlier,
        )

    parts = back_part(0, (), up_grad, out_grad)
    down_scattered = after(down_scattered, parts[0])
    down_moved = [
        lax.ppermute(
            down_scattered[:, s * units : (s + 1) * units],
            "tp",
            [(i, (i - s) % n) for i in range(n)],
        )
        for s in range(1, n)
    ]
    dq, dkv = back_part(1, parts, down_scattered)
    down_moved = [after(moved, dq) for moved in down_moved]
    dq, dkv = dq.reshape(hh, -1), dkv.reshape(2 * hh, -1)

    def share_of(position, dkv):
        part = slice(position * here, (position + 1) * here)
        return product("ct,dc->td", dkv[:, part], kv_full)

    to_later = [None] * (reach + 1)
    to_prior = [None] * (reach + 1)

    def send_shares(distance, dkv, sides="both"):
        for i, (j, use_later, use_prior) in enumerate(slots):
            to_right_here = use_later and j == distance and sides != "prior"
            to_left_here = use_prior and n - j == distance and sides != "later"
            if not (to_right_here or to_left_here):
                continue
            part = share_of(i + 1, dkv).astype(BF)
            zero = jnp.zeros_like(part)
            if to_right_here:
                to_later[j] = jnp.where(me + j < n, part, zero)
            if to_left_here:
                to_prior[n - j] = jnp.where(me + j >= n, part, zero)

    def joined(moving, share_here):
        return (moving.astype(F32) + share_here.astype(F32)).astype(BF)

    send_shares(reach, dkv)
    moving_right = lax.ppermute(to_later[reach], "tp", to_right)
    moving_left = lax.ppermute(to_prior[reach], "tp", to_left)
    dkv = after(dkv, to_later[reach], to_prior[reach], *down_moved)
    query_grad = product("td,ct->dc", normed, dq).astype(BF)
    kv_grad = product("td,ct->dc", normed_all, dkv).astype(BF)
    gates = (kv_grad, query_grad)
    if reach > 1:
        dkv = after(dkv, *gates)
        for distance in reversed(range(2, reach)):
            send_shares(distance, dkv)
        gates = (*gates, moving_right, moving_left)
    attn_grad = jnp.concatenate([query_grad, kv_grad, after(out_grad, *gates)], axis=1)
    attn_scattered = lax.psum_scatter(attn_grad, "fsdp", scatter_dimension=0, tiled=True)
    dkv, up_scattered = after(dkv, attn_grad), after(up_scattered, attn_grad)
    up_moved = [
        lax.ppermute(
            up_scattered[:, s * units : (s + 1) * units],
            "tp",
            [(i, (i - s) % n) for i in range(n)],
        )
        for s in range(1, n)
    ]
    for distance in reversed(range(2, reach)):
        moving_right = lax.ppermute(joined(moving_right, to_later[distance]), "tp", to_right)
        moving_left = lax.ppermute(joined(moving_left, to_prior[distance]), "tp", to_left)
    if reach > 1:
        send_shares(1, dkv, "later")
        moving_right = joined(moving_right, to_later[1])
        dkv, dq = after(dkv, moving_right), after(dq, moving_right)
        moving_right = lax.ppermute(moving_right, "tp", to_right)
    own_share = share_of(0, dkv) + product("ct,dc->td", dq, query_full)
    up_moved = [after(moved, own_share) for moved in up_moved]
    if reach > 1:
        dkv = after(dkv, *up_moved)
        send_shares(1, dkv, "prior")
        moving_right = after(moving_right, to_prior[1])
        moving_left = lax.ppermute(joined(moving_left, to_prior[1]), "tp", to_left)
    last_sent = [t for t in (own_share, to_prior[1]) if t is not None]
    grad_normed = own_share + moving_right.astype(F32) + moving_left.astype(F32)

    one_hat, one_rstd = xhat_of(x)
    grad_x, gain_one_part, shift_one_part = norm_back(grad_normed, one_hat, one_rstd, gain_one)
    input_grad = grad_middle + grad_x

    query_bias_part = jnp.sum(dq, axis=1, dtype=F32)
    value_bias_part = jnp.sum(dkv[hh:], axis=1, dtype=F32)
    vector_part = jnp.concatenate(
        [
            gain_one_part,
            shift_one_part,
            out_bias_part,
            gain_two_part,
            shift_two_part,
            down_bias_part,
        ]
    )
    up_bias_parts = jnp.take(up_bias_part.reshape(n, units), ring_order, axis=0).reshape(-1)
    small = jnp.concatenate([query_bias_part, value_bias_part, up_bias_parts, vector_part])

    def sum_over(value, axis):
        count = lax.axis_size(axis)
        if count & (count - 1):
            return lax.psum(value, axis)
        bit = 1
        while bit < count:
            value = value + lax.ppermute(value, axis, [(i, i ^ bit) for i in range(count)])
            bit *= 2
        return value

    def summed(scattered, moved):
        return sum((m.astype(F32) for m in moved), scattered[:, :units].astype(F32))

    down_weight_grad = summed(down_scattered, down_moved)
    up_weight_grad = summed(up_scattered, up_moved)
    attn_owned = by_owner(after(attn_scattered, *last_sent), n, 4)
    small = after(small, attn_owned)
    small = sum_over(sum_over(small, "tp"), "fsdp")
    attn_out = lax.psum_scatter(attn_owned, "tp", scatter_dimension=0, tiled=True).astype(F32)
    mixed = product("tf,df->td", after(active_units, attn_owned), down_full) + down_shift
    activations_out = ((middle + mixed) * valid_col).astype(BF)

    bias_size = (2 * cols + units) * n
    query_bias_grad, value_bias_grad, up_bias_grad = (
        lax.dynamic_slice_in_dim(small, start + me * size, size, 0)
        for start, size in ((0, cols), (hh, cols), (2 * hh, units))
    )
    own_vectors = lax.dynamic_slice_in_dim(
        small[bias_size:].reshape(6, width), lax.axis_index("fsdp") * share, share, 1
    )
    return (
        activations_out[None],
        input_grad[None],
        own_vectors[0:1],
        own_vectors[1:2],
        attn_out[None, :, :cols],
        query_bias_grad[None],
        attn_out[None, :, cols : 2 * cols],
        attn_out[None, :, 2 * cols : 3 * cols],
        value_bias_grad[None],
        attn_out[None, :, 3 * cols :],
        own_vectors[2:3],
        own_vectors[3:4],
        own_vectors[4:5],
        up_weight_grad[None],
        up_bias_grad[None],
        down_weight_grad[None],
        own_vectors[5:6],
    )


def solution(mesh):
    token = P("fsdp", "tp", None)
    vector, shift, matrix = P(None, "fsdp"), P(None, "tp"), P(None, "fsdp", "tp")
    in_specs = (
        token,
        P("fsdp", None),
        token,
        vector,
        vector,
        matrix,
        shift,
        matrix,
        matrix,
        shift,
        matrix,
        vector,
        vector,
        vector,
        matrix,
        shift,
        matrix,
        vector,
    )
    out_specs = (
        token,
        token,
        vector,
        vector,
        matrix,
        shift,
        matrix,
        matrix,
        shift,
        matrix,
        vector,
        vector,
        vector,
        matrix,
        shift,
        matrix,
        vector,
    )
    return jax.shard_map(local, mesh=mesh, in_specs=in_specs, out_specs=out_specs, check_vma=False)
```

```python
import functools
import math

import jax
import jax.numpy as jnp
from jax import lax
from jax.experimental import pallas as pl
from jax.experimental.pallas import tpu as pltpu
from jax.sharding import PartitionSpec as P

HEAD_DIM = 72
AUG = 8
PIC_MAX = 1024
MASKED = -1e30
BF = jnp.bfloat16
F32 = jnp.float32


def xhat_of(values):
    center = values - jnp.mean(values, axis=-1, keepdims=True)
    rstd = lax.rsqrt(jnp.mean(center * center, axis=-1, keepdims=True) + 1e-06)
    return center * rstd, rstd


def norm_back(dy, xhat, rstd, gain):
    dxhat = dy * gain
    grad = dxhat - jnp.mean(dxhat, axis=-1, keepdims=True)
    grad = (grad - xhat * jnp.mean(dxhat * xhat, axis=-1, keepdims=True)) * rstd
    return grad, jnp.sum(dy * xhat, axis=0), jnp.sum(dy, axis=0)


def gelu_tanh(values):
    return jax.nn.gelu(values, approximate=True)


def product(form, left, right):
    return jnp.einsum(form, left, right, preferred_element_type=F32)


def split3(values):
    high = lax.reduce_precision(values, 8, 7)
    rest = values - high
    mid = lax.reduce_precision(rest, 8, 7)
    return jnp.stack([high, mid, rest - mid], axis=0)


def after(value, *earlier):
    def kernel(*refs):
        pass

    return pl.pallas_call(
        kernel,
        in_specs=[pl.BlockSpec(memory_space=pl.ANY)] * (1 + len(earlier)),
        out_specs=pl.BlockSpec(memory_space=pl.ANY),
        out_shape=jax.ShapeDtypeStruct(value.shape, value.dtype),
        input_output_aliases={0: 0},
        compiler_params=pltpu.CompilerParams(vmem_limit_bytes=54 << 20),
        name="after",
    )(value, *earlier)


def copy_after(value, *earlier):
    def kernel(value_ref, *refs):
        refs[-1][...] = value_ref[...]

    vmem = pl.BlockSpec(memory_space=pltpu.VMEM)
    return pl.pallas_call(
        kernel,
        in_specs=[vmem] + [pl.BlockSpec(memory_space=pl.ANY)] * len(earlier),
        out_specs=vmem,
        out_shape=jax.ShapeDtypeStruct(value.shape, value.dtype),
        compiler_params=pltpu.CompilerParams(vmem_limit_bytes=54 << 20),
        name="copy_after",
    )(value, *earlier)


def slots_along_tp(piece, count, *earlier):
    slots = [piece]
    for distance in range(1, count):
        moved = lax.ppermute(piece, "tp", [(i, (i + distance) % count) for i in range(count)])
        slots.append(after(moved, *earlier) if earlier else moved)
    return slots


def by_owner(value, owners, kinds):
    rows, columns = value.shape
    size = columns // (owners * kinds)

    def kernel(value_ref, out_ref):
        for o in range(owners):
            pieces = [
                value_ref[:, (t * owners + o) * size : (t * owners + o + 1) * size]
                for t in range(kinds)
            ]
            out_ref[o] = jnp.concatenate(pieces, axis=1)

    vmem = pl.BlockSpec(memory_space=pltpu.VMEM)
    return pl.pallas_call(
        kernel,
        in_specs=[vmem],
        out_specs=vmem,
        out_shape=jax.ShapeDtypeStruct((owners, rows, kinds * size), value.dtype),
        compiler_params=pltpu.CompilerParams(vmem_limit_bytes=54 << 20),
        name="by_owner",
    )(value).reshape(owners * rows, kinds * size)


def norm_kernel(x_ref, gain_ref, shift_ref, *rest):
    values = x_ref[...].astype(F32)
    center = values - jnp.mean(values, axis=1, keepdims=True)
    spread = jnp.mean(center * center, axis=1, keepdims=True)
    result = center * lax.rsqrt(spread + 1e-06) * gain_ref[...] + shift_ref[...]
    rest[-1][...] = result.astype(BF)


def norm_slot(tokens, gain, shift, slot, slots, *into):
    here, width = tokens.shape
    block = math.gcd(here, 128)
    steps = here // block
    whole = pl.BlockSpec((1, width), lambda i: (0, 0))
    return pl.pallas_call(
        norm_kernel,
        grid=(steps,),
        in_specs=[pl.BlockSpec((block, width), lambda i: (i, 0)), whole, whole]
        + [pl.BlockSpec(memory_space=pl.ANY)] * len(into),
        out_specs=pl.BlockSpec((block, width), lambda i: (slot * steps + i, 0)),
        out_shape=jax.ShapeDtypeStruct((slots * here, width), BF),
        input_output_aliases={3: 0} if into else {},
        cost_estimate=pl.CostEstimate(
            flops=10 * here * width, bytes_accessed=4 * here * width, transcendentals=here
        ),
        compiler_params=pltpu.CompilerParams(vmem_limit_bytes=54 << 20),
        name="norm_slot",
    )(tokens, gain[None], shift[None], *into)


def attend_kernel(
    count_ref, index_ref, q_ref, k_ref, v_ref, valid_ref, *rest, q_block, k_block, pair
):
    o_ref, lse_ref = rest[-2:]
    heads, rows, q_len = q_ref.shape
    chunks = k_ref.shape[2] // k_block
    dim = rows - AUG
    blocks = q_len // q_block
    jobs = [(b, h) for b in range(blocks) for h in range(heads)]

    def step(t, carry):
        out = []
        for (b, h), (top, acc) in zip(jobs, carry):
            q_part = q_ref[h, :, b * q_block : (b + 1) * q_block]
            starts = [index_ref[b * chunks + t * pair + u] * k_block for u in range(pair)]
            heres = [pl.ds(pl.multiple_of(start, k_block), k_block) for start in starts]
            k_part = jnp.concatenate([k_ref[h, :, here] for here in heres], axis=1)
            v_part = jnp.concatenate([v_ref[h, :, here] for here in heres], axis=1)
            scores = lax.dot_general(
                k_part, q_part, (((0,), (0,)), ((), ())), preferred_element_type=F32
            )
            higher = jnp.maximum(top, jnp.max(scores, axis=0, keepdims=True))
            weights = jnp.exp2(scores - higher).astype(BF)
            acc = acc * jnp.exp2(top - higher) + jnp.dot(
                v_part, weights, preferred_element_type=F32
            )
            out.append((higher, acc))
        return tuple(out)

    first = tuple(
        (jnp.full((1, q_block), MASKED, F32), jnp.zeros((rows, q_block), F32)) for _ in jobs
    )
    final = lax.fori_loop(0, count_ref[0], step, first)
    for (b, h), (top, acc) in zip(jobs, final):
        cols = slice(b * q_block, (b + 1) * q_block)
        live = valid_ref[:, cols] > 0
        total = jnp.where(live, acc[dim : dim + 1], 1.0)
        o_ref[h, :, cols] = jnp.where(live, acc[:dim] / total, 0.0).astype(BF)
        lse_ref[h, :, cols] = jnp.where(live, top + jnp.log2(total), 0.0)


def attend(
    q_aug, k_aug, v_aug, valid, counts, indices, q_block, k_block, pair, group, part, parts, *earlier
):
    heads, rows, q_len = q_aug.shape
    heads = heads // parts
    base = part * (heads // group)
    k_len = k_aug.shape[2]
    dim = rows - AUG
    spec = lambda r, n: pl.BlockSpec((group, r, n), lambda g, *_: (g + base, 0, 0))
    out = lambda r, n: pl.BlockSpec((group, r, n), lambda g, *_: (g, 0, 0))
    return pl.pallas_call(
        functools.partial(attend_kernel, q_block=q_block, k_block=k_block, pair=pair),
        grid_spec=pltpu.PrefetchScalarGridSpec(
            num_scalar_prefetch=2,
            grid=(heads // group,),
            in_specs=[
                spec(rows, q_len),
                spec(rows, k_len),
                spec(rows, k_len),
                pl.BlockSpec((1, q_len), lambda g, *_: (0, 0)),
            ]
            + [pl.BlockSpec(memory_space=pl.ANY)] * len(earlier),
            out_specs=[out(dim, q_len), out(1, q_len)],
        ),
        out_shape=[
            jax.ShapeDtypeStruct((heads, dim, q_len), BF),
            jax.ShapeDtypeStruct((heads, 1, q_len), F32),
        ],
        compiler_params=pltpu.CompilerParams(vmem_limit_bytes=54 << 20),
        cost_estimate=pl.CostEstimate(
            flops=4 * heads * rows * q_len * k_len,
            bytes_accessed=4 * heads * rows * (q_len + k_len),
            transcendentals=heads * q_len * k_len // 2,
        ),
        name="attend",
    )(counts, indices, q_aug, k_aug, v_aug, valid, *earlier)


def attend_back_kernel(
    count_ref, index_ref, q_ref, k_ref, v_ref, g_ref, *rest, q_block, k_block, pair
):
    dq_ref, dkv_ref, dk_acc, dv_acc = rest[-4:]
    heads, rows, q_len = q_ref.shape
    chunks = k_ref.shape[2] // k_block
    dim = rows - AUG
    blocks = q_len // q_block
    jobs = [(b, h) for b in range(blocks) for h in range(heads)]
    dk_acc[...] = jnp.zeros_like(dk_acc)
    dv_acc[...] = jnp.zeros_like(dv_acc)

    def step(t, carry):
        out, sums = [], []
        for (b, h), dq in zip(jobs, carry):
            cols = slice(b * q_block, (b + 1) * q_block)
            q_part, g_part = q_ref[h, :, cols], g_ref[h, :, cols]
            starts = [index_ref[b * chunks + t * pair + u] * k_block for u in range(pair)]
            heres = [pl.ds(pl.multiple_of(start, k_block), k_block) for start in starts]
            k_part = jnp.concatenate([k_ref[h, :, here] for here in heres], axis=1)
            v_part = jnp.concatenate([v_ref[h, :, here] for here in heres], axis=1)
            scores = lax.dot_general(
                k_part, q_part, (((0,), (0,)), ((), ())), preferred_element_type=F32
            )
            probs = jnp.exp2(scores)
            dprobs = lax.dot_general(
                v_part, g_part, (((0,), (0,)), ((), ())), preferred_element_type=F32
            )
            dscores = (probs * dprobs).astype(BF)
            dq += jnp.dot(k_part, dscores, preferred_element_type=F32)
            dk = lax.dot_general(
                q_part, dscores, (((1,), (1,)), ((), ())), preferred_element_type=F32
            )
            dv = lax.dot_general(
                g_part, probs.astype(BF), (((1,), (1,)), ((), ())), preferred_element_type=F32
            )
            sums.append((h, heres, dk, dv))
            out.append(dq)
        for h, heres, dk, dv in sums:
            for u, here in enumerate(heres):
                dk_acc[h, :, here] += dk[:, u * k_block : (u + 1) * k_block]
                dv_acc[h, :, here] += dv[:, u * k_block : (u + 1) * k_block]
        return tuple(out)

    first = tuple(jnp.zeros((rows, q_block), F32) for _ in jobs)
    final = lax.fori_loop(0, count_ref[0], step, first)
    for (b, h), dq in zip(jobs, final):
        cols = slice(b * q_block, (b + 1) * q_block)
        dq_ref[h, :, cols] = (dq[:dim] * dim**-0.5).astype(BF)
    for h in range(heads):
        dkv_ref[0, h] = (dk_acc[h, :dim, :] * math.log(2.0)).astype(BF)
        dkv_ref[1, h] = dv_acc[h, :dim, :].astype(BF)


def attend_back(
    q_aug, k_aug, v_aug, g_aug, counts, indices, q_block, k_block, pair, group, part, parts, before, *earlier
):
    heads, rows, q_len = q_aug.shape
    k_len = k_aug.shape[2]
    dim = rows - AUG
    base = part * (heads // parts // group)
    spec = lambda r, n: pl.BlockSpec((group, r, n), lambda g, *_: (g + base, 0, 0))
    earlier = (*before, *earlier)
    return pl.pallas_call(
        functools.partial(attend_back_kernel, q_block=q_block, k_block=k_block, pair=pair),
        grid_spec=pltpu.PrefetchScalarGridSpec(
            num_scalar_prefetch=2,
            grid=(heads // parts // group,),
            in_specs=[spec(rows, q_len), spec(rows, k_len), spec(rows, k_len), spec(rows, q_len)]
            + [pl.BlockSpec(memory_space=pl.ANY)] * len(earlier),
            out_specs=[
                spec(dim, q_len),
                pl.BlockSpec((2, group, dim, k_len), lambda g, *_: (0, g + base, 0, 0)),
            ],
            scratch_shapes=[
                pltpu.VMEM((group, rows, k_len), F32),
                pltpu.VMEM((group, rows, k_len), F32),
            ],
        ),
        out_shape=[
            jax.ShapeDtypeStruct((heads, dim, q_len), BF),
            jax.ShapeDtypeStruct((2, heads, dim, k_len), BF),
        ],
        compiler_params=pltpu.CompilerParams(vmem_limit_bytes=54 << 20),
        cost_estimate=pl.CostEstimate(
            flops=10 * heads * rows * q_len * k_len,
            bytes_accessed=8 * heads * rows * (q_len + k_len),
            transcendentals=heads * q_len * k_len // 2,
        ),
        input_output_aliases={6 + i: i for i in range(len(before))},
        name="attend_back",
    )(counts, indices, q_aug, k_aug, v_aug, g_aug, *earlier)


def local(
    activations,
    lengths,
    cotangent,
    ln1_gain,
    ln1_bias,
    query_weight,
    query_bias,
    key_weight,
    value_weight,
    value_bias,
    out_weight,
    out_bias,
    ln2_gain,
    ln2_bias,
    up_weight,
    up_bias,
    down_weight,
    down_bias,
):
    n = lax.axis_size("tp")
    me = lax.axis_index("tp")
    _, here, width = activations.shape
    total_len = here * n
    pics = lengths.shape[1]
    cols = query_weight.shape[2]
    units = up_weight.shape[2]
    heads = cols * n // HEAD_DIM
    hh = cols * n
    reach = min(n - 1, -(-(PIC_MAX - 1) // here))
    scale = HEAD_DIM**-0.5

    x_own = activations[0]
    to_left = [(i, i - 1) for i in range(1, n)]
    to_right = [(i, i + 1) for i in range(n - 1)]
    ends = jnp.cumsum(lengths[0])
    positions = jnp.arange(total_len, dtype=jnp.int32)
    segment = jnp.sum((positions[:, None] >= ends[None, :]).astype(jnp.int32), axis=1)
    own_seg = lax.dynamic_slice_in_dim(segment, me * here, here, 0)
    bias_piece = jnp.concatenate([query_bias[0], value_bias[0], up_bias[0]])
    bias_terms = split3(bias_piece).astype(BF).reshape(-1)
    bias_rows = -(-bias_terms.shape[0] // (3 * cols * 8)) * 8
    bias_terms = jnp.pad(bias_terms, (0, bias_rows * 3 * cols - bias_terms.shape[0]))
    attn_piece = jnp.concatenate([query_weight[0], key_weight[0], value_weight[0]], axis=1)
    attn_piece = jnp.concatenate([attn_piece, bias_terms.reshape(bias_rows, 3 * cols)], axis=0)
    attn_parts = lax.all_gather(attn_piece, "tp", axis=0)
    vectors = jnp.concatenate([ln1_gain, ln1_bias, out_bias, ln2_gain, ln2_bias, down_bias], axis=0)
    vectors = lax.all_gather(vectors, "fsdp", axis=1, tiled=True)
    gain_one, shift_one, out_shift, gain_two, shift_two, down_shift = vectors
    slots = []
    for j in range(1, n):
        use_later, use_prior = j <= reach, n - j <= reach
        if use_later or use_prior:
            slots.append((j, use_later, use_prior))
    slots.sort(key=lambda slot: min(slot[0], n - slot[0]))

    key_segs = [own_seg]
    for j, use_later, use_prior in slots:
        seg = lax.dynamic_slice_in_dim(segment, ((me + j) % n) * here, here, 0)
        there = jnp.where(me + j < n, use_later, use_prior)
        key_segs.append(jnp.where(there, seg, pics))
    key_seg = jnp.concatenate(key_segs)
    k_len = key_seg.shape[0]
    valid = (own_seg < pics).astype(F32)
    valid_col = valid[:, None]
    q_block = min(512, here)
    k_block = min(256, here)
    pair = 2 if k_len % (2 * k_block) == 0 else 1
    picture = jnp.arange(pics, dtype=jnp.int32)
    q_has = jnp.any(own_seg.reshape(-1, q_block, 1) == picture, axis=1)
    k_has = jnp.any(key_seg.reshape(-1, k_block, 1) == picture, axis=1)
    active = jnp.any(q_has[:, None, :] & k_has[None, :, :], axis=2)
    used = jnp.sum(active.astype(jnp.int32), axis=1, keepdims=True)
    counts = -(-jnp.max(used, axis=0) // pair)
    place = jnp.where(
        active,
        jnp.cumsum(active.astype(jnp.int32), axis=1) - 1,
        used + jnp.cumsum(1 - active.astype(jnp.int32), axis=1) - 1,
    )
    chunk_ids = jnp.arange(active.shape[1], dtype=jnp.int32)
    hit = place[:, :, None] == chunk_ids[None, None, :]
    indices = jnp.sum(jnp.where(hit, chunk_ids[None, :, None], 0), axis=1).reshape(-1)

    q_mask = jnp.concatenate(
        [
            jnp.where(own_seg[None, :] == picture[:, None], 0.0, MASKED),
            jnp.full((1, here), MASKED, F32),
        ],
        axis=0,
    )
    k_mask = jnp.concatenate(
        [(key_seg[None, :] == picture[:, None]), (key_seg >= pics)[None, :]], axis=0
    ).astype(BF)
    spare = AUG - (pics + 1) - 3
    k_added = jnp.concatenate(
        [k_mask, jnp.ones((3, k_len), BF), jnp.zeros((spare, k_len), BF)], axis=0
    )
    v_added = jnp.concatenate([jnp.ones((3, k_len), BF), jnp.zeros((AUG - 3, k_len), BF)], axis=0)

    grad_two = cotangent[0].astype(F32) * valid_col
    grad_mixed = grad_two.astype(BF)
    down_bias_part = jnp.sum(grad_mixed, axis=0, dtype=F32)
    later = [x_own, lax.ppermute(x_own, "tp", to_left)]
    prior = [x_own, lax.ppermute(x_own, "tp", to_right)]
    attn_parts = after(
        attn_parts,
        vectors,
        counts,
        indices,
        k_added,
        q_mask,
        down_bias_part,
        grad_mixed,
        later[1],
        prior[1],
    )
    share = query_weight.shape[1]
    all_biases = jnp.sum(
        attn_parts[:, share:]
        .reshape(n, -1)[:, : 3 * bias_piece.shape[0]]
        .reshape(n, 3, -1)
        .astype(F32),
        axis=1,
    )
    query_shift = all_biases[:, :cols].reshape(-1)
    value_shift = all_biases[:, cols : 2 * cols].reshape(-1)
    ring_order = (me - jnp.arange(n)) % n
    up_shift = jnp.take(all_biases[:, 2 * cols :], ring_order, axis=0).reshape(-1)
    wide_piece = jnp.concatenate([out_weight[0], up_weight[0]], axis=1)
    wide_slots = slots_along_tp(
        copy_after(wide_piece, attn_parts, up_shift, query_shift, value_shift), n
    )
    later[1], prior[1] = after(later[1], *wide_slots[1:]), after(prior[1], *wide_slots[1:])
    for _ in range(reach - 1):
        later.append(lax.ppermute(later[-1], "tp", to_left))
        prior.append(lax.ppermute(prior[-1], "tp", to_right))

    slot_count = 1 + len(slots)
    normed_all = norm_slot(x_own, gain_one, shift_one, 0, slot_count)
    for position, (j, use_later, use_prior) in enumerate(slots):
        if use_later and use_prior:
            tokens = jnp.where(me + j < n, later[j], prior[n - j])
        else:
            tokens = later[j] if use_later else prior[n - j]
        if min(j, n - j) == 1:
            normed_all = norm_slot(
                tokens, gain_one, shift_one, position + 1, slot_count, normed_all
            )
        else:
            normed_all = norm_slot(
                tokens, gain_one, shift_one, position + 1, slot_count, normed_all
            )
    first_down = copy_after(down_weight[0], later[-1], prior[-1])

    def widen(body, added):
        body = body.reshape(heads, HEAD_DIM, body.shape[-1])
        added = jnp.broadcast_to(added, (heads, AUG, body.shape[-1]))
        return jnp.concatenate([body, added.astype(BF)], axis=1)

    attn_shard = jnp.concatenate(
        [attn_parts[o, :share, t * cols : (t + 1) * cols] for t in range(3) for o in range(n)],
        axis=1,
    )
    attn_full = lax.all_gather(attn_shard, "fsdp", axis=0, tiled=True)
    out_slots = jnp.take(jnp.stack([s[:, :cols] for s in wide_slots]), ring_order, axis=0)
    wide_shard = jnp.concatenate(
        [out_slots[o] for o in range(n)] + [s[:, cols:] for s in wide_slots], axis=1
    )
    wide_full = lax.all_gather(wide_shard, "fsdp", axis=0, tiled=True)
    out_full, up_full = wide_full[:, :hh], wide_full[:, hh:]

    query_full = attn_full[:, :hh]
    key_full = attn_full[:, hh : 2 * hh]
    value_full = attn_full[:, 2 * hh : 3 * hh]
    kv_full = attn_full[:, hh : 3 * hh]

    x = x_own.astype(F32)
    normed = normed_all[:here]
    queries = (
        (product("td,dc->ct", normed, query_full) + query_shift[:, None])
        * (scale * math.log2(math.e))
    ).astype(BF)
    q_rest = jnp.zeros((AUG - (pics + 1), here), F32)
    q_aug = widen(queries, jnp.concatenate([q_mask, q_rest], axis=0))

    keys = product("td,dc->ct", normed_all, key_full).astype(BF)
    values = product("td,dc->ct", normed_all, value_full) + value_shift[:, None]
    k_aug = after(widen(keys, k_added))
    v_aug = after(widen(values.astype(BF), v_added))
    down_slots = slots_along_tp(first_down, n, k_aug, v_aug)
    group = 4 if heads % 8 == 0 else 1
    down_shard = jnp.concatenate(down_slots, axis=1)
    down_full = lax.all_gather(down_shard, "fsdp", axis=0, tiled=True)
    attended, log_total = attend(
        q_aug,
        k_aug,
        v_aug,
        valid[None, :],
        counts,
        indices,
        q_block,
        k_block,
        pair,
        group,
        0,
        1,
        down_shard,
    )
    flat = attended.reshape(hh, here)
    middle = x + (product("ct,dc->td", flat, out_full) + out_shift)

    two_hat, two_rstd = xhat_of(middle)
    normed_two = (two_hat * gain_two + shift_two).astype(BF)
    hidden = product("td,df->tf", normed_two, up_full) + up_shift
    active_units, gelu_pull = jax.vjp(gelu_tanh, hidden)
    active_units = active_units.astype(BF)

    down_grad = product("td,tf->df", grad_mixed, active_units).astype(BF)
    down_scattered = lax.psum_scatter(down_grad, "fsdp", scatter_dimension=0, tiled=True)
    back_mixed = after(grad_mixed, down_grad)
    grad_hidden = gelu_pull(product("td,df->tf", back_mixed, down_full))[0].astype(BF)
    up_bias_part = jnp.sum(grad_hidden, axis=0, dtype=F32)
    up_grad = product("td,tf->df", normed_two, grad_hidden).astype(BF)
    grad_normed_two = product("tf,df->td", grad_hidden, up_full)
    grad_middle, gain_two_part, shift_two_part = norm_back(
        grad_normed_two, two_hat, two_rstd, gain_two
    )
    grad_middle = grad_two + grad_middle
    grad_branch = grad_middle.astype(BF)
    out_bias_part = jnp.sum(grad_branch, axis=0, dtype=F32)
    out_grad = product("td,ct->dc", grad_branch, flat).astype(BF)
    up_scattered = lax.psum_scatter(up_grad, "fsdp", scatter_dimension=0, tiled=True)

    grad_attended = product("td,dc->ct", grad_branch, out_full).astype(BF)
    grad_attended = grad_attended * valid.astype(BF)
    grad_heads = grad_attended.reshape(heads, HEAD_DIM, here)
    delta = jnp.sum(grad_heads.astype(F32) * attended.astype(F32), axis=1)
    g_added = jnp.concatenate(
        [
            jnp.moveaxis(split3(-delta), 0, 1),
            jnp.zeros((heads, AUG - 3, here), F32),
        ],
        axis=1,
    )
    g_aug = widen(grad_attended, g_added)
    q_added = jnp.concatenate(
        [
            jnp.broadcast_to(q_mask, (heads, pics + 1, here)),
            jnp.moveaxis(split3(-log_total[:, 0]), 0, 1),
            jnp.zeros((heads, spare, here), F32),
        ],
        axis=1,
    )
    q_aug_back = widen(queries, q_added)
    def back_part(part, before, *earlier):
        return attend_back(
            q_aug_back,
            k_aug,
            v_aug,
            g_aug,
            counts,
            indices,
            q_block,
            k_block,
            pair,
            group,
            part,
            2,
            before,
            *earlier,
        )

    parts = back_part(0, (), up_grad, out_grad)
    down_scattered = after(down_scattered, parts[0])
    down_moved = [
        lax.ppermute(
            down_scattered[:, s * units : (s + 1) * units],
            "tp",
            [(i, (i - s) % n) for i in range(n)],
        )
        for s in range(1, n)
    ]
    dq, dkv = back_part(1, parts, down_scattered)
    down_moved = [after(moved, dq) for moved in down_moved]
    dq, dkv = dq.reshape(hh, -1), dkv.reshape(2 * hh, -1)

    def share_of(position, dkv):
        part = slice(position * here, (position + 1) * here)
        return product("ct,dc->td", dkv[:, part], kv_full)

    to_later = [None] * (reach + 1)
    to_prior = [None] * (reach + 1)

    def send_shares(distance, dkv, sides="both"):
        for i, (j, use_later, use_prior) in enumerate(slots):
            to_right_here = use_later and j == distance and sides != "prior"
            to_left_here = use_prior and n - j == distance and sides != "later"
            if not (to_right_here or to_left_here):
                continue
            part = share_of(i + 1, dkv).astype(BF)
            zero = jnp.zeros_like(part)
            if to_right_here:
                to_later[j] = jnp.where(me + j < n, part, zero)
            if to_left_here:
                to_prior[n - j] = jnp.where(me + j >= n, part, zero)

    def joined(moving, share_here):
        return (moving.astype(F32) + share_here.astype(F32)).astype(BF)

    send_shares(reach, dkv)
    moving_right = lax.ppermute(to_later[reach], "tp", to_right)
    moving_left = lax.ppermute(to_prior[reach], "tp", to_left)
    dkv = after(dkv, to_later[reach], to_prior[reach], *down_moved)
    query_grad = product("td,ct->dc", normed, dq).astype(BF)
    kv_grad = product("td,ct->dc", normed_all, dkv).astype(BF)
    gates = (kv_grad, query_grad)
    if reach > 1:
        dkv = after(dkv, *gates)
        for distance in reversed(range(2, reach)):
            send_shares(distance, dkv)
        gates = (*gates, moving_right, moving_left)
    attn_grad = jnp.concatenate([query_grad, kv_grad, after(out_grad, *gates)], axis=1)
    attn_scattered = lax.psum_scatter(attn_grad, "fsdp", scatter_dimension=0, tiled=True)
    dkv, up_scattered = after(dkv, attn_grad), after(up_scattered, attn_grad)
    up_moved = [
        lax.ppermute(
            up_scattered[:, s * units : (s + 1) * units],
            "tp",
            [(i, (i - s) % n) for i in range(n)],
        )
        for s in range(1, n)
    ]
    for distance in reversed(range(2, reach)):
        moving_right = lax.ppermute(joined(moving_right, to_later[distance]), "tp", to_right)
        moving_left = lax.ppermute(joined(moving_left, to_prior[distance]), "tp", to_left)
    if reach > 1:
        send_shares(1, dkv, "later")
        moving_right = joined(moving_right, to_later[1])
        dkv = after(dkv, moving_right, *up_moved[:1])
        dq = after(dq, moving_right, *up_moved[1:2])
        moving_right = lax.ppermute(moving_right, "tp", to_right)
    own_share = share_of(0, dkv) + product("ct,dc->td", dq, query_full)
    if reach > 1:
        dkv = after(dkv, own_share)
        send_shares(1, dkv, "prior")
        moving_right = after(moving_right, to_prior[1])
        moving_left = lax.ppermute(joined(moving_left, to_prior[1]), "tp", to_left)
    last_sent = [t for t in (own_share, to_prior[1], *up_moved) if t is not None]
    grad_normed = own_share + moving_right.astype(F32) + moving_left.astype(F32)

    one_hat, one_rstd = xhat_of(x)
    grad_x, gain_one_part, shift_one_part = norm_back(grad_normed, one_hat, one_rstd, gain_one)
    input_grad = grad_middle + grad_x

    query_bias_part = jnp.sum(dq, axis=1, dtype=F32)
    value_bias_part = jnp.sum(dkv[hh:], axis=1, dtype=F32)
    vector_part = jnp.concatenate(
        [
            gain_one_part,
            shift_one_part,
            out_bias_part,
            gain_two_part,
            shift_two_part,
            down_bias_part,
        ]
    )
    up_bias_parts = jnp.take(up_bias_part.reshape(n, units), ring_order, axis=0).reshape(-1)
    small = jnp.concatenate([query_bias_part, value_bias_part, up_bias_parts, vector_part])

    def sum_over(value, axis):
        count = lax.axis_size(axis)
        if count & (count - 1):
            return lax.psum(value, axis)
        bit = 1
        while bit < count:
            value = value + lax.ppermute(value, axis, [(i, i ^ bit) for i in range(count)])
            bit *= 2
        return value

    def summed(scattered, moved):
        return sum((m.astype(F32) for m in moved), scattered[:, :units].astype(F32))

    down_weight_grad = summed(down_scattered, down_moved)
    up_weight_grad = summed(up_scattered, up_moved)
    attn_owned = by_owner(after(attn_scattered, *last_sent), n, 4)
    small = after(small, attn_owned)
    small = sum_over(sum_over(small, "tp"), "fsdp")
    attn_out = lax.psum_scatter(attn_owned, "tp", scatter_dimension=0, tiled=True).astype(F32)
    mixed = product("tf,df->td", after(active_units, attn_owned), down_full) + down_shift
    activations_out = ((middle + mixed) * valid_col).astype(BF)

    bias_size = (2 * cols + units) * n
    query_bias_grad, value_bias_grad, up_bias_grad = (
        lax.dynamic_slice_in_dim(small, start + me * size, size, 0)
        for start, size in ((0, cols), (hh, cols), (2 * hh, units))
    )
    own_vectors = lax.dynamic_slice_in_dim(
        small[bias_size:].reshape(6, width), lax.axis_index("fsdp") * share, share, 1
    )
    return (
        activations_out[None],
        input_grad[None],
        own_vectors[0:1],
        own_vectors[1:2],
        attn_out[None, :, :cols],
        query_bias_grad[None],
        attn_out[None, :, cols : 2 * cols],
        attn_out[None, :, 2 * cols : 3 * cols],
        value_bias_grad[None],
        attn_out[None, :, 3 * cols :],
        own_vectors[2:3],
        own_vectors[3:4],
        own_vectors[4:5],
        up_weight_grad[None],
        up_bias_grad[None],
        down_weight_grad[None],
        own_vectors[5:6],
    )


def solution(mesh):
    token = P("fsdp", "tp", None)
    vector, shift, matrix = P(None, "fsdp"), P(None, "tp"), P(None, "fsdp", "tp")
    in_specs = (
        token,
        P("fsdp", None),
        token,
        vector,
        vector,
        matrix,
        shift,
        matrix,
        matrix,
        shift,
        matrix,
        vector,
        vector,
        vector,
        matrix,
        shift,
        matrix,
        vector,
    )
    out_specs = (
        token,
        token,
        vector,
        vector,
        matrix,
        shift,
        matrix,
        matrix,
        shift,
        matrix,
        vector,
        vector,
        vector,
        matrix,
        shift,
        matrix,
        vector,
    )
    return jax.shard_map(local, mesh=mesh, in_specs=in_specs, out_specs=out_specs, check_vma=False)
```

```python
import functools
import math

import jax
import jax.numpy as jnp
from jax import lax
from jax.experimental import pallas as pl
from jax.experimental.pallas import tpu as pltpu
from jax.sharding import PartitionSpec as P

HEAD_DIM = 72
AUG = 8
PIC_MAX = 1024
MASKED = -1e30
BF = jnp.bfloat16
F32 = jnp.float32


def xhat_of(values):
    center = values - jnp.mean(values, axis=-1, keepdims=True)
    rstd = lax.rsqrt(jnp.mean(center * center, axis=-1, keepdims=True) + 1e-06)
    return center * rstd, rstd


def norm_back(dy, xhat, rstd, gain):
    dxhat = dy * gain
    grad = dxhat - jnp.mean(dxhat, axis=-1, keepdims=True)
    grad = (grad - xhat * jnp.mean(dxhat * xhat, axis=-1, keepdims=True)) * rstd
    return grad, jnp.sum(dy * xhat, axis=0), jnp.sum(dy, axis=0)


def gelu_tanh(values):
    return jax.nn.gelu(values, approximate=True)


def product(form, left, right):
    return jnp.einsum(form, left, right, preferred_element_type=F32)


def split3(values):
    high = lax.reduce_precision(values, 8, 7)
    rest = values - high
    mid = lax.reduce_precision(rest, 8, 7)
    return jnp.stack([high, mid, rest - mid], axis=0)


def after(value, *earlier):
    def kernel(*refs):
        pass

    return pl.pallas_call(
        kernel,
        in_specs=[pl.BlockSpec(memory_space=pl.ANY)] * (1 + len(earlier)),
        out_specs=pl.BlockSpec(memory_space=pl.ANY),
        out_shape=jax.ShapeDtypeStruct(value.shape, value.dtype),
        input_output_aliases={0: 0},
        compiler_params=pltpu.CompilerParams(vmem_limit_bytes=54 << 20),
        name="after",
    )(value, *earlier)


def copy_after(value, *earlier):
    def kernel(value_ref, *refs):
        refs[-1][...] = value_ref[...]

    vmem = pl.BlockSpec(memory_space=pltpu.VMEM)
    return pl.pallas_call(
        kernel,
        in_specs=[vmem] + [pl.BlockSpec(memory_space=pl.ANY)] * len(earlier),
        out_specs=vmem,
        out_shape=jax.ShapeDtypeStruct(value.shape, value.dtype),
        compiler_params=pltpu.CompilerParams(vmem_limit_bytes=54 << 20),
        name="copy_after",
    )(value, *earlier)


def slots_along_tp(piece, count, *earlier):
    slots = [piece]
    for distance in range(1, count):
        moved = lax.ppermute(piece, "tp", [(i, (i + distance) % count) for i in range(count)])
        slots.append(after(moved, *earlier) if earlier else moved)
    return slots


def by_owner(value, owners, kinds):
    rows, columns = value.shape
    size = columns // (owners * kinds)

    def kernel(value_ref, out_ref):
        for o in range(owners):
            pieces = [
                value_ref[:, (t * owners + o) * size : (t * owners + o + 1) * size]
                for t in range(kinds)
            ]
            out_ref[o] = jnp.concatenate(pieces, axis=1)

    vmem = pl.BlockSpec(memory_space=pltpu.VMEM)
    return pl.pallas_call(
        kernel,
        in_specs=[vmem],
        out_specs=vmem,
        out_shape=jax.ShapeDtypeStruct((owners, rows, kinds * size), value.dtype),
        compiler_params=pltpu.CompilerParams(vmem_limit_bytes=54 << 20),
        name="by_owner",
    )(value).reshape(owners * rows, kinds * size)


def norm_kernel(x_ref, gain_ref, shift_ref, *rest):
    values = x_ref[...].astype(F32)
    center = values - jnp.mean(values, axis=1, keepdims=True)
    spread = jnp.mean(center * center, axis=1, keepdims=True)
    result = center * lax.rsqrt(spread + 1e-06) * gain_ref[...] + shift_ref[...]
    rest[-1][...] = result.astype(BF)


def norm_slot(tokens, gain, shift, slot, slots, *into):
    here, width = tokens.shape
    block = math.gcd(here, 128)
    steps = here // block
    whole = pl.BlockSpec((1, width), lambda i: (0, 0))
    return pl.pallas_call(
        norm_kernel,
        grid=(steps,),
        in_specs=[pl.BlockSpec((block, width), lambda i: (i, 0)), whole, whole]
        + [pl.BlockSpec(memory_space=pl.ANY)] * len(into),
        out_specs=pl.BlockSpec((block, width), lambda i: (slot * steps + i, 0)),
        out_shape=jax.ShapeDtypeStruct((slots * here, width), BF),
        input_output_aliases={3: 0} if into else {},
        cost_estimate=pl.CostEstimate(
            flops=10 * here * width, bytes_accessed=4 * here * width, transcendentals=here
        ),
        compiler_params=pltpu.CompilerParams(vmem_limit_bytes=54 << 20),
        name="norm_slot",
    )(tokens, gain[None], shift[None], *into)


def attend_kernel(
    count_ref, index_ref, q_ref, k_ref, v_ref, valid_ref, *rest, q_block, k_block, pair
):
    o_ref, lse_ref = rest[-2:]
    heads, rows, q_len = q_ref.shape
    chunks = k_ref.shape[2] // k_block
    dim = rows - AUG
    blocks = q_len // q_block
    jobs = [(b, h) for b in range(blocks) for h in range(heads)]

    def step(t, carry):
        out = []
        for (b, h), (top, acc) in zip(jobs, carry):
            q_part = q_ref[h, :, b * q_block : (b + 1) * q_block]
            if pair == chunks:
                k_part, v_part = k_ref[h], v_ref[h]
            else:
                starts = [index_ref[b * chunks + t * pair + u] * k_block for u in range(pair)]
                heres = [pl.ds(pl.multiple_of(start, k_block), k_block) for start in starts]
                k_part = jnp.concatenate([k_ref[h, :, here] for here in heres], axis=1)
                v_part = jnp.concatenate([v_ref[h, :, here] for here in heres], axis=1)
            scores = lax.dot_general(
                k_part, q_part, (((0,), (0,)), ((), ())), preferred_element_type=F32
            )
            higher = jnp.maximum(top, jnp.max(scores, axis=0, keepdims=True))
            weights = jnp.exp2(scores - higher).astype(BF)
            acc = acc * jnp.exp2(top - higher) + jnp.dot(
                v_part, weights, preferred_element_type=F32
            )
            out.append((higher, acc))
        return tuple(out)

    first = tuple(
        (jnp.full((1, q_block), MASKED, F32), jnp.zeros((rows, q_block), F32)) for _ in jobs
    )
    final = step(0, first) if pair == chunks else lax.fori_loop(0, count_ref[0], step, first)
    for (b, h), (top, acc) in zip(jobs, final):
        cols = slice(b * q_block, (b + 1) * q_block)
        live = valid_ref[:, cols] > 0
        total = jnp.where(live, acc[dim : dim + 1], 1.0)
        o_ref[h, :, cols] = jnp.where(live, acc[:dim] / total, 0.0).astype(BF)
        lse_ref[h, :, cols] = jnp.where(live, top + jnp.log2(total), 0.0)


def attend(
    q_aug, k_aug, v_aug, valid, counts, indices, q_block, k_block, pair, group, part, parts, *earlier
):
    heads, rows, q_len = q_aug.shape
    heads = heads // parts
    base = part * (heads // group)
    k_len = k_aug.shape[2]
    dim = rows - AUG
    spec = lambda r, n: pl.BlockSpec((group, r, n), lambda g, *_: (g + base, 0, 0))
    out = lambda r, n: pl.BlockSpec((group, r, n), lambda g, *_: (g, 0, 0))
    return pl.pallas_call(
        functools.partial(attend_kernel, q_block=q_block, k_block=k_block, pair=pair),
        grid_spec=pltpu.PrefetchScalarGridSpec(
            num_scalar_prefetch=2,
            grid=(heads // group,),
            in_specs=[
                spec(rows, q_len),
                spec(rows, k_len),
                spec(rows, k_len),
                pl.BlockSpec((1, q_len), lambda g, *_: (0, 0)),
            ]
            + [pl.BlockSpec(memory_space=pl.ANY)] * len(earlier),
            out_specs=[out(dim, q_len), out(1, q_len)],
        ),
        out_shape=[
            jax.ShapeDtypeStruct((heads, dim, q_len), BF),
            jax.ShapeDtypeStruct((heads, 1, q_len), F32),
        ],
        compiler_params=pltpu.CompilerParams(vmem_limit_bytes=54 << 20),
        cost_estimate=pl.CostEstimate(
            flops=4 * heads * rows * q_len * k_len,
            bytes_accessed=4 * heads * rows * (q_len + k_len),
            transcendentals=heads * q_len * k_len // 2,
        ),
        name="attend",
    )(counts, indices, q_aug, k_aug, v_aug, valid, *earlier)


def attend_back_kernel(
    count_ref, index_ref, q_ref, k_ref, v_ref, g_ref, *rest, q_block, k_block, pair
):
    dq_ref, dkv_ref, dk_acc, dv_acc = rest[-4:]
    heads, rows, q_len = q_ref.shape
    chunks = k_ref.shape[2] // k_block
    dim = rows - AUG
    blocks = q_len // q_block
    jobs = [(b, h) for b in range(blocks) for h in range(heads)]
    dk_acc[...] = jnp.zeros_like(dk_acc)
    dv_acc[...] = jnp.zeros_like(dv_acc)

    def step(t, carry):
        out, sums = [], []
        for (b, h), dq in zip(jobs, carry):
            cols = slice(b * q_block, (b + 1) * q_block)
            q_part, g_part = q_ref[h, :, cols], g_ref[h, :, cols]
            if pair == chunks:
                k_part, v_part = k_ref[h], v_ref[h]
            else:
                starts = [index_ref[b * chunks + t * pair + u] * k_block for u in range(pair)]
                heres = [pl.ds(pl.multiple_of(start, k_block), k_block) for start in starts]
                k_part = jnp.concatenate([k_ref[h, :, here] for here in heres], axis=1)
                v_part = jnp.concatenate([v_ref[h, :, here] for here in heres], axis=1)
            scores = lax.dot_general(
                k_part, q_part, (((0,), (0,)), ((), ())), preferred_element_type=F32
            )
            probs = jnp.exp2(scores)
            dprobs = lax.dot_general(
                v_part, g_part, (((0,), (0,)), ((), ())), preferred_element_type=F32
            )
            dscores = (probs * dprobs).astype(BF)
            dq += jnp.dot(k_part, dscores, preferred_element_type=F32)
            dk = lax.dot_general(
                q_part, dscores, (((1,), (1,)), ((), ())), preferred_element_type=F32
            )
            dv = lax.dot_general(
                g_part, probs.astype(BF), (((1,), (1,)), ((), ())), preferred_element_type=F32
            )
            if pair == chunks:
                heres = [slice(u * k_block, (u + 1) * k_block) for u in range(pair)]
            sums.append((h, heres, dk, dv))
            out.append(dq)
        for h, heres, dk, dv in sums:
            for u, here in enumerate(heres):
                dk_acc[h, :, here] += dk[:, u * k_block : (u + 1) * k_block]
                dv_acc[h, :, here] += dv[:, u * k_block : (u + 1) * k_block]
        return tuple(out)

    first = tuple(jnp.zeros((rows, q_block), F32) for _ in jobs)
    final = step(0, first) if pair == chunks else lax.fori_loop(0, count_ref[0], step, first)
    for (b, h), dq in zip(jobs, final):
        cols = slice(b * q_block, (b + 1) * q_block)
        dq_ref[h, :, cols] = (dq[:dim] * dim**-0.5).astype(BF)
    for h in range(heads):
        dkv_ref[0, h] = (dk_acc[h, :dim, :] * math.log(2.0)).astype(BF)
        dkv_ref[1, h] = dv_acc[h, :dim, :].astype(BF)


def attend_back(
    q_aug, k_aug, v_aug, g_aug, counts, indices, q_block, k_block, pair, group, part, parts, before, *earlier
):
    heads, rows, q_len = q_aug.shape
    k_len = k_aug.shape[2]
    dim = rows - AUG
    base = part * (heads // parts // group)
    spec = lambda r, n: pl.BlockSpec((group, r, n), lambda g, *_: (g + base, 0, 0))
    earlier = (*before, *earlier)
    return pl.pallas_call(
        functools.partial(attend_back_kernel, q_block=q_block, k_block=k_block, pair=pair),
        grid_spec=pltpu.PrefetchScalarGridSpec(
            num_scalar_prefetch=2,
            grid=(heads // parts // group,),
            in_specs=[spec(rows, q_len), spec(rows, k_len), spec(rows, k_len), spec(rows, q_len)]
            + [pl.BlockSpec(memory_space=pl.ANY)] * len(earlier),
            out_specs=[
                spec(dim, q_len),
                pl.BlockSpec((2, group, dim, k_len), lambda g, *_: (0, g + base, 0, 0)),
            ],
            scratch_shapes=[
                pltpu.VMEM((group, rows, k_len), F32),
                pltpu.VMEM((group, rows, k_len), F32),
            ],
        ),
        out_shape=[
            jax.ShapeDtypeStruct((heads, dim, q_len), BF),
            jax.ShapeDtypeStruct((2, heads, dim, k_len), BF),
        ],
        compiler_params=pltpu.CompilerParams(vmem_limit_bytes=54 << 20),
        cost_estimate=pl.CostEstimate(
            flops=10 * heads * rows * q_len * k_len,
            bytes_accessed=8 * heads * rows * (q_len + k_len),
            transcendentals=heads * q_len * k_len // 2,
        ),
        input_output_aliases={6 + i: i for i in range(len(before))},
        name="attend_back",
    )(counts, indices, q_aug, k_aug, v_aug, g_aug, *earlier)


def local(
    activations,
    lengths,
    cotangent,
    ln1_gain,
    ln1_bias,
    query_weight,
    query_bias,
    key_weight,
    value_weight,
    value_bias,
    out_weight,
    out_bias,
    ln2_gain,
    ln2_bias,
    up_weight,
    up_bias,
    down_weight,
    down_bias,
):
    n = lax.axis_size("tp")
    me = lax.axis_index("tp")
    _, here, width = activations.shape
    total_len = here * n
    pics = lengths.shape[1]
    cols = query_weight.shape[2]
    units = up_weight.shape[2]
    heads = cols * n // HEAD_DIM
    hh = cols * n
    reach = min(n - 1, -(-(PIC_MAX - 1) // here))
    scale = HEAD_DIM**-0.5

    x_own = activations[0]
    to_left = [(i, i - 1) for i in range(1, n)]
    to_right = [(i, i + 1) for i in range(n - 1)]
    ends = jnp.cumsum(lengths[0])
    positions = jnp.arange(total_len, dtype=jnp.int32)
    segment = jnp.sum((positions[:, None] >= ends[None, :]).astype(jnp.int32), axis=1)
    own_seg = lax.dynamic_slice_in_dim(segment, me * here, here, 0)
    bias_piece = jnp.concatenate([query_bias[0], value_bias[0], up_bias[0]])
    bias_terms = split3(bias_piece).astype(BF).reshape(-1)
    bias_rows = -(-bias_terms.shape[0] // (3 * cols * 8)) * 8
    bias_terms = jnp.pad(bias_terms, (0, bias_rows * 3 * cols - bias_terms.shape[0]))
    attn_piece = jnp.concatenate([query_weight[0], key_weight[0], value_weight[0]], axis=1)
    attn_piece = jnp.concatenate([attn_piece, bias_terms.reshape(bias_rows, 3 * cols)], axis=0)
    attn_parts = lax.all_gather(attn_piece, "tp", axis=0)
    vectors = jnp.concatenate([ln1_gain, ln1_bias, out_bias, ln2_gain, ln2_bias, down_bias], axis=0)
    vectors = lax.all_gather(vectors, "fsdp", axis=1, tiled=True)
    gain_one, shift_one, out_shift, gain_two, shift_two, down_shift = vectors
    slots = []
    for j in range(1, n):
        use_later, use_prior = j <= reach, n - j <= reach
        if use_later or use_prior:
            slots.append((j, use_later, use_prior))
    slots.sort(key=lambda slot: min(slot[0], n - slot[0]))

    key_segs = [own_seg]
    for j, use_later, use_prior in slots:
        seg = lax.dynamic_slice_in_dim(segment, ((me + j) % n) * here, here, 0)
        there = jnp.where(me + j < n, use_later, use_prior)
        key_segs.append(jnp.where(there, seg, pics))
    key_seg = jnp.concatenate(key_segs)
    k_len = key_seg.shape[0]
    valid = (own_seg < pics).astype(F32)
    valid_col = valid[:, None]
    q_block = min(512, here)
    k_block = min(256, here)
    pair = k_len // k_block
    picture = jnp.arange(pics, dtype=jnp.int32)
    q_has = jnp.any(own_seg.reshape(-1, q_block, 1) == picture, axis=1)
    k_has = jnp.any(key_seg.reshape(-1, k_block, 1) == picture, axis=1)
    active = jnp.any(q_has[:, None, :] & k_has[None, :, :], axis=2)
    used = jnp.sum(active.astype(jnp.int32), axis=1, keepdims=True)
    counts = -(-jnp.max(used, axis=0) // pair)
    place = jnp.where(
        active,
        jnp.cumsum(active.astype(jnp.int32), axis=1) - 1,
        used + jnp.cumsum(1 - active.astype(jnp.int32), axis=1) - 1,
    )
    chunk_ids = jnp.arange(active.shape[1], dtype=jnp.int32)
    hit = place[:, :, None] == chunk_ids[None, None, :]
    indices = jnp.sum(jnp.where(hit, chunk_ids[None, :, None], 0), axis=1).reshape(-1)

    q_mask = jnp.concatenate(
        [
            jnp.where(own_seg[None, :] == picture[:, None], 0.0, MASKED),
            jnp.full((1, here), MASKED, F32),
        ],
        axis=0,
    )
    k_mask = jnp.concatenate(
        [(key_seg[None, :] == picture[:, None]), (key_seg >= pics)[None, :]], axis=0
    ).astype(BF)
    spare = AUG - (pics + 1) - 3
    k_added = jnp.concatenate(
        [k_mask, jnp.ones((3, k_len), BF), jnp.zeros((spare, k_len), BF)], axis=0
    )
    v_added = jnp.concatenate([jnp.ones((3, k_len), BF), jnp.zeros((AUG - 3, k_len), BF)], axis=0)

    grad_two = cotangent[0].astype(F32) * valid_col
    grad_mixed = grad_two.astype(BF)
    down_bias_part = jnp.sum(grad_mixed, axis=0, dtype=F32)
    later = [x_own, lax.ppermute(x_own, "tp", to_left)]
    prior = [x_own, lax.ppermute(x_own, "tp", to_right)]
    attn_parts = after(
        attn_parts,
        vectors,
        counts,
        indices,
        k_added,
        q_mask,
        down_bias_part,
        grad_mixed,
        later[1],
        prior[1],
    )
    share = query_weight.shape[1]
    all_biases = jnp.sum(
        attn_parts[:, share:]
        .reshape(n, -1)[:, : 3 * bias_piece.shape[0]]
        .reshape(n, 3, -1)
        .astype(F32),
        axis=1,
    )
    query_shift = all_biases[:, :cols].reshape(-1)
    value_shift = all_biases[:, cols : 2 * cols].reshape(-1)
    ring_order = (me - jnp.arange(n)) % n
    up_shift = jnp.take(all_biases[:, 2 * cols :], ring_order, axis=0).reshape(-1)
    wide_piece = jnp.concatenate([out_weight[0], up_weight[0]], axis=1)
    wide_slots = slots_along_tp(
        copy_after(wide_piece, attn_parts, up_shift, query_shift, value_shift), n
    )
    later[1], prior[1] = after(later[1], *wide_slots[1:]), after(prior[1], *wide_slots[1:])
    for _ in range(reach - 1):
        later.append(lax.ppermute(later[-1], "tp", to_left))
        prior.append(lax.ppermute(prior[-1], "tp", to_right))

    slot_count = 1 + len(slots)
    normed_all = norm_slot(x_own, gain_one, shift_one, 0, slot_count)
    for position, (j, use_later, use_prior) in enumerate(slots):
        if use_later and use_prior:
            tokens = jnp.where(me + j < n, later[j], prior[n - j])
        else:
            tokens = later[j] if use_later else prior[n - j]
        if min(j, n - j) == 1:
            normed_all = norm_slot(
                tokens, gain_one, shift_one, position + 1, slot_count, normed_all
            )
        else:
            normed_all = norm_slot(
                tokens, gain_one, shift_one, position + 1, slot_count, normed_all
            )

    def widen(body, added):
        body = body.reshape(heads, HEAD_DIM, body.shape[-1])
        added = jnp.broadcast_to(added, (heads, AUG, body.shape[-1]))
        return jnp.concatenate([body, added.astype(BF)], axis=1)

    attn_shard = jnp.concatenate(
        [attn_parts[o, :share, t * cols : (t + 1) * cols] for t in range(3) for o in range(n)],
        axis=1,
    )
    attn_full = lax.all_gather(attn_shard, "fsdp", axis=0, tiled=True)
    out_slots = jnp.take(jnp.stack([s[:, :cols] for s in wide_slots]), ring_order, axis=0)
    wide_shard = jnp.concatenate(
        [out_slots[o] for o in range(n)] + [s[:, cols:] for s in wide_slots], axis=1
    )
    wide_full = lax.all_gather(wide_shard, "fsdp", axis=0, tiled=True)
    out_full, up_full = wide_full[:, :hh], wide_full[:, hh:]

    query_full = attn_full[:, :hh]
    key_full = attn_full[:, hh : 2 * hh]
    value_full = attn_full[:, 2 * hh : 3 * hh]
    kv_full = attn_full[:, hh : 3 * hh]

    x = x_own.astype(F32)
    normed = normed_all[:here]
    queries = (
        (product("td,dc->ct", normed, query_full) + query_shift[:, None])
        * (scale * math.log2(math.e))
    ).astype(BF)
    first_down = copy_after(down_weight[0], later[-1], prior[-1], queries)
    q_rest = jnp.zeros((AUG - (pics + 1), here), F32)
    q_aug = widen(queries, jnp.concatenate([q_mask, q_rest], axis=0))

    keys = product("td,dc->ct", normed_all, key_full).astype(BF)
    values = product("td,dc->ct", normed_all, value_full) + value_shift[:, None]
    k_aug = after(widen(keys, k_added))
    v_aug = after(widen(values.astype(BF), v_added))
    down_slots = slots_along_tp(first_down, n, k_aug, v_aug)
    group = 2 if heads % 4 == 0 else 1
    down_shard = jnp.concatenate(down_slots, axis=1)
    down_full = lax.all_gather(down_shard, "fsdp", axis=0, tiled=True)
    attended, log_total = attend(
        q_aug,
        k_aug,
        v_aug,
        valid[None, :],
        counts,
        indices,
        q_block,
        k_block,
        pair,
        group,
        0,
        1,
        down_shard,
    )
    flat = attended.reshape(hh, here)
    middle = x + (product("ct,dc->td", flat, out_full) + out_shift)

    two_hat, two_rstd = xhat_of(middle)
    normed_two = (two_hat * gain_two + shift_two).astype(BF)
    hidden = product("td,df->tf", normed_two, up_full) + up_shift
    active_units, gelu_pull = jax.vjp(gelu_tanh, hidden)
    active_units = active_units.astype(BF)

    down_grad = product("td,tf->df", grad_mixed, active_units).astype(BF)
    down_scattered = lax.psum_scatter(down_grad, "fsdp", scatter_dimension=0, tiled=True)
    back_mixed = after(grad_mixed, down_grad)
    grad_hidden = gelu_pull(product("td,df->tf", back_mixed, down_full))[0].astype(BF)
    up_bias_part = jnp.sum(grad_hidden, axis=0, dtype=F32)
    up_grad = product("td,tf->df", normed_two, grad_hidden).astype(BF)
    grad_normed_two = product("tf,df->td", grad_hidden, up_full)
    grad_middle, gain_two_part, shift_two_part = norm_back(
        grad_normed_two, two_hat, two_rstd, gain_two
    )
    grad_middle = grad_two + grad_middle
    grad_branch = grad_middle.astype(BF)
    out_bias_part = jnp.sum(grad_branch, axis=0, dtype=F32)
    out_grad = product("td,ct->dc", grad_branch, flat).astype(BF)
    up_scattered = lax.psum_scatter(up_grad, "fsdp", scatter_dimension=0, tiled=True)

    grad_attended = product("td,dc->ct", grad_branch, out_full).astype(BF)
    grad_attended = grad_attended * valid.astype(BF)
    grad_heads = grad_attended.reshape(heads, HEAD_DIM, here)
    delta = jnp.sum(grad_heads.astype(F32) * attended.astype(F32), axis=1)
    g_added = jnp.concatenate(
        [
            jnp.moveaxis(split3(-delta), 0, 1),
            jnp.zeros((heads, AUG - 3, here), F32),
        ],
        axis=1,
    )
    g_aug = widen(grad_attended, g_added)
    q_added = jnp.concatenate(
        [
            jnp.broadcast_to(q_mask, (heads, pics + 1, here)),
            jnp.moveaxis(split3(-log_total[:, 0]), 0, 1),
            jnp.zeros((heads, spare, here), F32),
        ],
        axis=1,
    )
    q_aug_back = widen(queries, q_added)
    def back_part(part, before, *earlier):
        return attend_back(
            q_aug_back,
            k_aug,
            v_aug,
            g_aug,
            counts,
            indices,
            q_block,
            k_block,
            pair,
            group,
            part,
            2,
            before,
            *earlier,
        )

    parts = back_part(0, (), up_grad, out_grad)
    down_scattered = after(down_scattered, parts[0])
    down_moved = [
        lax.ppermute(
            down_scattered[:, s * units : (s + 1) * units],
            "tp",
            [(i, (i - s) % n) for i in range(n)],
        )
        for s in range(1, n)
    ]
    dq, dkv = back_part(1, parts, down_scattered)
    down_moved = [after(moved, dq) for moved in down_moved]
    dq, dkv = dq.reshape(hh, -1), dkv.reshape(2 * hh, -1)

    def share_of(position, dkv):
        part = slice(position * here, (position + 1) * here)
        return product("ct,dc->td", dkv[:, part], kv_full)

    to_later = [None] * (reach + 1)
    to_prior = [None] * (reach + 1)

    def send_shares(distance, dkv, sides="both"):
        for i, (j, use_later, use_prior) in enumerate(slots):
            to_right_here = use_later and j == distance and sides != "prior"
            to_left_here = use_prior and n - j == distance and sides != "later"
            if not (to_right_here or to_left_here):
                continue
            part = share_of(i + 1, dkv).astype(BF)
            zero = jnp.zeros_like(part)
            if to_right_here:
                to_later[j] = jnp.where(me + j < n, part, zero)
            if to_left_here:
                to_prior[n - j] = jnp.where(me + j >= n, part, zero)

    def joined(moving, share_here):
        return (moving.astype(F32) + share_here.astype(F32)).astype(BF)

    send_shares(reach, dkv)
    moving_right = lax.ppermute(to_later[reach], "tp", to_right)
    moving_left = lax.ppermute(to_prior[reach], "tp", to_left)
    dkv = after(dkv, to_later[reach], to_prior[reach], *down_moved)
    query_grad = product("td,ct->dc", normed, dq).astype(BF)
    kv_grad = product("td,ct->dc", normed_all, dkv).astype(BF)
    gates = (kv_grad, query_grad)
    if reach > 1:
        dkv = after(dkv, *gates)
        for distance in reversed(range(2, reach)):
            send_shares(distance, dkv)
        gates = (*gates, moving_right, moving_left)
    attn_grad = jnp.concatenate([query_grad, kv_grad, after(out_grad, *gates)], axis=1)
    attn_scattered = lax.psum_scatter(attn_grad, "fsdp", scatter_dimension=0, tiled=True)
    dkv, up_scattered = after(dkv, attn_grad), after(up_scattered, attn_grad)
    up_moved = [
        lax.ppermute(
            up_scattered[:, s * units : (s + 1) * units],
            "tp",
            [(i, (i - s) % n) for i in range(n)],
        )
        for s in range(1, n)
    ]
    for distance in reversed(range(2, reach)):
        moving_right = lax.ppermute(joined(moving_right, to_later[distance]), "tp", to_right)
        moving_left = lax.ppermute(joined(moving_left, to_prior[distance]), "tp", to_left)
    if reach > 1:
        send_shares(1, dkv, "later")
        moving_right = joined(moving_right, to_later[1])
        dkv = after(dkv, moving_right, *up_moved[:1])
        dq = after(dq, moving_right, *up_moved[1:2])
        moving_right = lax.ppermute(moving_right, "tp", to_right)
    own_share = share_of(0, dkv) + product("ct,dc->td", dq, query_full)
    if reach > 1:
        dkv = after(dkv, own_share)
        send_shares(1, dkv, "prior")
        moving_right = after(moving_right, to_prior[1])
        moving_left = lax.ppermute(joined(moving_left, to_prior[1]), "tp", to_left)
    last_sent = [t for t in (own_share, to_prior[1], *up_moved) if t is not None]
    grad_normed = own_share + moving_right.astype(F32) + moving_left.astype(F32)

    one_hat, one_rstd = xhat_of(x)
    grad_x, gain_one_part, shift_one_part = norm_back(grad_normed, one_hat, one_rstd, gain_one)
    input_grad = grad_middle + grad_x

    query_bias_part = jnp.sum(dq, axis=1, dtype=F32)
    value_bias_part = jnp.sum(dkv[hh:], axis=1, dtype=F32)
    vector_part = jnp.concatenate(
        [
            gain_one_part,
            shift_one_part,
            out_bias_part,
            gain_two_part,
            shift_two_part,
            down_bias_part,
        ]
    )
    up_bias_parts = jnp.take(up_bias_part.reshape(n, units), ring_order, axis=0).reshape(-1)
    small = jnp.concatenate([query_bias_part, value_bias_part, up_bias_parts, vector_part])

    def sum_over(value, axis):
        count = lax.axis_size(axis)
        if count & (count - 1):
            return lax.psum(value, axis)
        bit = 1
        while bit < count:
            value = value + lax.ppermute(value, axis, [(i, i ^ bit) for i in range(count)])
            bit *= 2
        return value

    def summed(scattered, moved):
        return sum((m.astype(F32) for m in moved), scattered[:, :units].astype(F32))

    down_weight_grad = summed(down_scattered, down_moved)
    up_weight_grad = summed(up_scattered, up_moved)
    attn_owned = by_owner(after(attn_scattered, *last_sent), n, 4)
    small = after(small, attn_owned)
    small = sum_over(sum_over(small, "tp"), "fsdp")
    attn_out = lax.psum_scatter(attn_owned, "tp", scatter_dimension=0, tiled=True).astype(F32)
    mixed = product("tf,df->td", after(active_units, attn_owned), down_full) + down_shift
    activations_out = ((middle + mixed) * valid_col).astype(BF)

    bias_size = (2 * cols + units) * n
    query_bias_grad, value_bias_grad, up_bias_grad = (
        lax.dynamic_slice_in_dim(small, start + me * size, size, 0)
        for start, size in ((0, cols), (hh, cols), (2 * hh, units))
    )
    own_vectors = lax.dynamic_slice_in_dim(
        small[bias_size:].reshape(6, width), lax.axis_index("fsdp") * share, share, 1
    )
    return (
        activations_out[None],
        input_grad[None],
        own_vectors[0:1],
        own_vectors[1:2],
        attn_out[None, :, :cols],
        query_bias_grad[None],
        attn_out[None, :, cols : 2 * cols],
        attn_out[None, :, 2 * cols : 3 * cols],
        value_bias_grad[None],
        attn_out[None, :, 3 * cols :],
        own_vectors[2:3],
        own_vectors[3:4],
        own_vectors[4:5],
        up_weight_grad[None],
        up_bias_grad[None],
        down_weight_grad[None],
        own_vectors[5:6],
    )


def solution(mesh):
    token = P("fsdp", "tp", None)
    vector, shift, matrix = P(None, "fsdp"), P(None, "tp"), P(None, "fsdp", "tp")
    in_specs = (
        token,
        P("fsdp", None),
        token,
        vector,
        vector,
        matrix,
        shift,
        matrix,
        matrix,
        shift,
        matrix,
        vector,
        vector,
        vector,
        matrix,
        shift,
        matrix,
        vector,
    )
    out_specs = (
        token,
        token,
        vector,
        vector,
        matrix,
        shift,
        matrix,
        matrix,
        shift,
        matrix,
        vector,
        vector,
        vector,
        matrix,
        shift,
        matrix,
        vector,
    )
    return jax.shard_map(local, mesh=mesh, in_specs=in_specs, out_specs=out_specs, check_vma=False)
```

```python
import functools
import math

import jax
import jax.numpy as jnp
from jax import lax
from jax.experimental import pallas as pl
from jax.experimental.pallas import tpu as pltpu
from jax.sharding import PartitionSpec as P

HEAD_DIM = 72
AUG = 8
PIC_MAX = 1024
MASKED = -1e30
BF = jnp.bfloat16
F32 = jnp.float32


def xhat_of(values):
    center = values - jnp.mean(values, axis=-1, keepdims=True)
    rstd = lax.rsqrt(jnp.mean(center * center, axis=-1, keepdims=True) + 1e-06)
    return center * rstd, rstd


def norm_back(dy, xhat, rstd, gain):
    dxhat = dy * gain
    grad = dxhat - jnp.mean(dxhat, axis=-1, keepdims=True)
    grad = (grad - xhat * jnp.mean(dxhat * xhat, axis=-1, keepdims=True)) * rstd
    return grad, jnp.sum(dy * xhat, axis=0), jnp.sum(dy, axis=0)


def gelu_tanh(values):
    return jax.nn.gelu(values, approximate=True)


def product(form, left, right):
    return jnp.einsum(form, left, right, preferred_element_type=F32)


def split3(values):
    high = lax.reduce_precision(values, 8, 7)
    rest = values - high
    mid = lax.reduce_precision(rest, 8, 7)
    return jnp.stack([high, mid, rest - mid], axis=0)


def after(value, *earlier):
    def kernel(*refs):
        pass

    return pl.pallas_call(
        kernel,
        in_specs=[pl.BlockSpec(memory_space=pl.ANY)] * (1 + len(earlier)),
        out_specs=pl.BlockSpec(memory_space=pl.ANY),
        out_shape=jax.ShapeDtypeStruct(value.shape, value.dtype),
        input_output_aliases={0: 0},
        compiler_params=pltpu.CompilerParams(vmem_limit_bytes=54 << 20),
        name="after",
    )(value, *earlier)


def copy_after(value, *earlier):
    def kernel(value_ref, *refs):
        refs[-1][...] = value_ref[...]

    vmem = pl.BlockSpec(memory_space=pltpu.VMEM)
    return pl.pallas_call(
        kernel,
        in_specs=[vmem] + [pl.BlockSpec(memory_space=pl.ANY)] * len(earlier),
        out_specs=vmem,
        out_shape=jax.ShapeDtypeStruct(value.shape, value.dtype),
        compiler_params=pltpu.CompilerParams(vmem_limit_bytes=54 << 20),
        name="copy_after",
    )(value, *earlier)


def slots_along_tp(piece, count, *earlier):
    slots = [piece]
    for distance in range(1, count):
        moved = lax.ppermute(piece, "tp", [(i, (i + distance) % count) for i in range(count)])
        slots.append(after(moved, *earlier) if earlier else moved)
    return slots


def by_owner(value, owners, kinds):
    rows, columns = value.shape
    size = columns // (owners * kinds)

    def kernel(value_ref, out_ref):
        for o in range(owners):
            pieces = [
                value_ref[:, (t * owners + o) * size : (t * owners + o + 1) * size]
                for t in range(kinds)
            ]
            out_ref[o] = jnp.concatenate(pieces, axis=1)

    vmem = pl.BlockSpec(memory_space=pltpu.VMEM)
    return pl.pallas_call(
        kernel,
        in_specs=[vmem],
        out_specs=vmem,
        out_shape=jax.ShapeDtypeStruct((owners, rows, kinds * size), value.dtype),
        compiler_params=pltpu.CompilerParams(vmem_limit_bytes=54 << 20),
        name="by_owner",
    )(value).reshape(owners * rows, kinds * size)


def norm_kernel(x_ref, gain_ref, shift_ref, *rest):
    values = x_ref[...].astype(F32)
    center = values - jnp.mean(values, axis=1, keepdims=True)
    spread = jnp.mean(center * center, axis=1, keepdims=True)
    result = center * lax.rsqrt(spread + 1e-06) * gain_ref[...] + shift_ref[...]
    rest[-1][...] = result.astype(BF)


def norm_slot(tokens, gain, shift, slot, slots, *into):
    here, width = tokens.shape
    block = math.gcd(here, 128)
    steps = here // block
    whole = pl.BlockSpec((1, width), lambda i: (0, 0))
    return pl.pallas_call(
        norm_kernel,
        grid=(steps,),
        in_specs=[pl.BlockSpec((block, width), lambda i: (i, 0)), whole, whole]
        + [pl.BlockSpec(memory_space=pl.ANY)] * len(into),
        out_specs=pl.BlockSpec((block, width), lambda i: (slot * steps + i, 0)),
        out_shape=jax.ShapeDtypeStruct((slots * here, width), BF),
        input_output_aliases={3: 0} if into else {},
        cost_estimate=pl.CostEstimate(
            flops=10 * here * width, bytes_accessed=4 * here * width, transcendentals=here
        ),
        compiler_params=pltpu.CompilerParams(vmem_limit_bytes=54 << 20),
        name="norm_slot",
    )(tokens, gain[None], shift[None], *into)


def attend_kernel(
    count_ref, index_ref, q_ref, k_ref, v_ref, valid_ref, *rest, q_block, k_block, pair
):
    o_ref, lse_ref = rest[-2:]
    heads, rows, q_len = q_ref.shape
    chunks = k_ref.shape[2] // k_block
    dim = rows - AUG
    blocks = q_len // q_block
    jobs = [(b, h) for b in range(blocks) for h in range(heads)]

    def step(t, carry):
        out = []
        for (b, h), (top, acc) in zip(jobs, carry):
            q_part = q_ref[h, :, b * q_block : (b + 1) * q_block]
            if pair == chunks:
                k_part, v_part = k_ref[h], v_ref[h]
            else:
                starts = [index_ref[b * chunks + t * pair + u] * k_block for u in range(pair)]
                heres = [pl.ds(pl.multiple_of(start, k_block), k_block) for start in starts]
                k_part = jnp.concatenate([k_ref[h, :, here] for here in heres], axis=1)
                v_part = jnp.concatenate([v_ref[h, :, here] for here in heres], axis=1)
            scores = lax.dot_general(
                k_part, q_part, (((0,), (0,)), ((), ())), preferred_element_type=F32
            )
            higher = jnp.maximum(top, jnp.max(scores, axis=0, keepdims=True))
            weights = jnp.exp2(scores - higher).astype(BF)
            acc = acc * jnp.exp2(top - higher) + jnp.dot(
                v_part, weights, preferred_element_type=F32
            )
            out.append((higher, acc))
        return tuple(out)

    first = tuple(
        (jnp.full((1, q_block), MASKED, F32), jnp.zeros((rows, q_block), F32)) for _ in jobs
    )
    final = step(0, first) if pair == chunks else lax.fori_loop(0, count_ref[0], step, first)
    for (b, h), (top, acc) in zip(jobs, final):
        cols = slice(b * q_block, (b + 1) * q_block)
        live = valid_ref[:, cols] > 0
        total = jnp.where(live, acc[dim : dim + 1], 1.0)
        o_ref[h, :, cols] = jnp.where(live, acc[:dim] / total, 0.0).astype(BF)
        lse_ref[h, :, cols] = jnp.where(live, top + jnp.log2(total), 0.0)


def attend(
    q_aug, k_aug, v_aug, valid, counts, indices, q_block, k_block, pair, group, part, parts, *earlier
):
    heads, rows, q_len = q_aug.shape
    heads = heads // parts
    base = part * (heads // group)
    k_len = k_aug.shape[2]
    dim = rows - AUG
    spec = lambda r, n: pl.BlockSpec((group, r, n), lambda g, *_: (g + base, 0, 0))
    out = lambda r, n: pl.BlockSpec((group, r, n), lambda g, *_: (g, 0, 0))
    return pl.pallas_call(
        functools.partial(attend_kernel, q_block=q_block, k_block=k_block, pair=pair),
        grid_spec=pltpu.PrefetchScalarGridSpec(
            num_scalar_prefetch=2,
            grid=(heads // group,),
            in_specs=[
                spec(rows, q_len),
                spec(rows, k_len),
                spec(rows, k_len),
                pl.BlockSpec((1, q_len), lambda g, *_: (0, 0)),
            ]
            + [pl.BlockSpec(memory_space=pl.ANY)] * len(earlier),
            out_specs=[out(dim, q_len), out(1, q_len)],
        ),
        out_shape=[
            jax.ShapeDtypeStruct((heads, dim, q_len), BF),
            jax.ShapeDtypeStruct((heads, 1, q_len), F32),
        ],
        compiler_params=pltpu.CompilerParams(vmem_limit_bytes=54 << 20),
        cost_estimate=pl.CostEstimate(
            flops=4 * heads * rows * q_len * k_len,
            bytes_accessed=4 * heads * rows * (q_len + k_len),
            transcendentals=heads * q_len * k_len // 2,
        ),
        name="attend",
    )(counts, indices, q_aug, k_aug, v_aug, valid, *earlier)


def attend_back_kernel(
    count_ref, index_ref, q_ref, k_ref, v_ref, g_ref, *rest, q_block, k_block, pair
):
    dq_ref, dkv_ref, dk_acc, dv_acc = rest[-4:]
    heads, rows, q_len = q_ref.shape
    chunks = k_ref.shape[2] // k_block
    dim = rows - AUG
    blocks = q_len // q_block
    jobs = [(b, h) for b in range(blocks) for h in range(heads)]
    dk_acc[...] = jnp.zeros_like(dk_acc)
    dv_acc[...] = jnp.zeros_like(dv_acc)

    def step(t, carry):
        out, sums = [], []
        for (b, h), dq in zip(jobs, carry):
            cols = slice(b * q_block, (b + 1) * q_block)
            q_part, g_part = q_ref[h, :, cols], g_ref[h, :, cols]
            if pair == chunks:
                k_part, v_part = k_ref[h], v_ref[h]
            else:
                starts = [index_ref[b * chunks + t * pair + u] * k_block for u in range(pair)]
                heres = [pl.ds(pl.multiple_of(start, k_block), k_block) for start in starts]
                k_part = jnp.concatenate([k_ref[h, :, here] for here in heres], axis=1)
                v_part = jnp.concatenate([v_ref[h, :, here] for here in heres], axis=1)
            scores = lax.dot_general(
                k_part, q_part, (((0,), (0,)), ((), ())), preferred_element_type=F32
            )
            probs = jnp.exp2(scores)
            dprobs = lax.dot_general(
                v_part, g_part, (((0,), (0,)), ((), ())), preferred_element_type=F32
            )
            dscores = (probs * dprobs).astype(BF)
            dq += jnp.dot(k_part, dscores, preferred_element_type=F32)
            dk = lax.dot_general(
                q_part, dscores, (((1,), (1,)), ((), ())), preferred_element_type=F32
            )
            dv = lax.dot_general(
                g_part, probs.astype(BF), (((1,), (1,)), ((), ())), preferred_element_type=F32
            )
            if pair == chunks:
                heres = [slice(u * k_block, (u + 1) * k_block) for u in range(pair)]
            sums.append((h, heres, dk, dv))
            out.append(dq)
        for h, heres, dk, dv in sums:
            for u, here in enumerate(heres):
                dk_acc[h, :, here] += dk[:, u * k_block : (u + 1) * k_block]
                dv_acc[h, :, here] += dv[:, u * k_block : (u + 1) * k_block]
        return tuple(out)

    first = tuple(jnp.zeros((rows, q_block), F32) for _ in jobs)
    final = step(0, first) if pair == chunks else lax.fori_loop(0, count_ref[0], step, first)
    for (b, h), dq in zip(jobs, final):
        cols = slice(b * q_block, (b + 1) * q_block)
        dq_ref[h, :, cols] = (dq[:dim] * dim**-0.5).astype(BF)
    for h in range(heads):
        dkv_ref[0, h] = (dk_acc[h, :dim, :] * math.log(2.0)).astype(BF)
        dkv_ref[1, h] = dv_acc[h, :dim, :].astype(BF)


def attend_back(
    q_aug, k_aug, v_aug, g_aug, counts, indices, q_block, k_block, pair, group, part, parts, before, *earlier
):
    heads, rows, q_len = q_aug.shape
    k_len = k_aug.shape[2]
    dim = rows - AUG
    base = part * (heads // parts // group)
    spec = lambda r, n: pl.BlockSpec((group, r, n), lambda g, *_: (g + base, 0, 0))
    earlier = (*before, *earlier)
    return pl.pallas_call(
        functools.partial(attend_back_kernel, q_block=q_block, k_block=k_block, pair=pair),
        grid_spec=pltpu.PrefetchScalarGridSpec(
            num_scalar_prefetch=2,
            grid=(heads // parts // group,),
            in_specs=[spec(rows, q_len), spec(rows, k_len), spec(rows, k_len), spec(rows, q_len)]
            + [pl.BlockSpec(memory_space=pl.ANY)] * len(earlier),
            out_specs=[
                spec(dim, q_len),
                pl.BlockSpec((2, group, dim, k_len), lambda g, *_: (0, g + base, 0, 0)),
            ],
            scratch_shapes=[
                pltpu.VMEM((group, rows, k_len), F32),
                pltpu.VMEM((group, rows, k_len), F32),
            ],
        ),
        out_shape=[
            jax.ShapeDtypeStruct((heads, dim, q_len), BF),
            jax.ShapeDtypeStruct((2, heads, dim, k_len), BF),
        ],
        compiler_params=pltpu.CompilerParams(vmem_limit_bytes=54 << 20),
        cost_estimate=pl.CostEstimate(
            flops=10 * heads * rows * q_len * k_len,
            bytes_accessed=8 * heads * rows * (q_len + k_len),
            transcendentals=heads * q_len * k_len // 2,
        ),
        input_output_aliases={6 + i: i for i in range(len(before))},
        name="attend_back",
    )(counts, indices, q_aug, k_aug, v_aug, g_aug, *earlier)


def local(
    activations,
    lengths,
    cotangent,
    ln1_gain,
    ln1_bias,
    query_weight,
    query_bias,
    key_weight,
    value_weight,
    value_bias,
    out_weight,
    out_bias,
    ln2_gain,
    ln2_bias,
    up_weight,
    up_bias,
    down_weight,
    down_bias,
):
    n = lax.axis_size("tp")
    me = lax.axis_index("tp")
    _, here, width = activations.shape
    total_len = here * n
    pics = lengths.shape[1]
    cols = query_weight.shape[2]
    units = up_weight.shape[2]
    heads = cols * n // HEAD_DIM
    hh = cols * n
    reach = min(n - 1, -(-(PIC_MAX - 1) // here))
    scale = HEAD_DIM**-0.5

    x_own = activations[0]
    to_left = [(i, i - 1) for i in range(1, n)]
    to_right = [(i, i + 1) for i in range(n - 1)]
    ends = jnp.cumsum(lengths[0])
    positions = jnp.arange(total_len, dtype=jnp.int32)
    segment = jnp.sum((positions[:, None] >= ends[None, :]).astype(jnp.int32), axis=1)
    own_seg = lax.dynamic_slice_in_dim(segment, me * here, here, 0)
    bias_piece = jnp.concatenate([query_bias[0], value_bias[0], up_bias[0]])
    bias_terms = split3(bias_piece).astype(BF).reshape(-1)
    bias_rows = -(-bias_terms.shape[0] // (3 * cols * 8)) * 8
    bias_terms = jnp.pad(bias_terms, (0, bias_rows * 3 * cols - bias_terms.shape[0]))
    attn_piece = jnp.concatenate([query_weight[0], key_weight[0], value_weight[0]], axis=1)
    attn_piece = jnp.concatenate([attn_piece, bias_terms.reshape(bias_rows, 3 * cols)], axis=0)
    attn_parts = lax.all_gather(attn_piece, "tp", axis=0)
    vectors = jnp.concatenate([ln1_gain, ln1_bias, out_bias, ln2_gain, ln2_bias, down_bias], axis=0)
    vectors = lax.all_gather(vectors, "fsdp", axis=1, tiled=True)
    gain_one, shift_one, out_shift, gain_two, shift_two, down_shift = vectors
    slots = []
    for j in range(1, n):
        use_later, use_prior = j <= reach, n - j <= reach
        if use_later or use_prior:
            slots.append((j, use_later, use_prior))
    slots.sort(key=lambda slot: min(slot[0], n - slot[0]))

    key_segs = [own_seg]
    for j, use_later, use_prior in slots:
        seg = lax.dynamic_slice_in_dim(segment, ((me + j) % n) * here, here, 0)
        there = jnp.where(me + j < n, use_later, use_prior)
        key_segs.append(jnp.where(there, seg, pics))
    key_seg = jnp.concatenate(key_segs)
    k_len = key_seg.shape[0]
    valid = (own_seg < pics).astype(F32)
    valid_col = valid[:, None]
    q_block = min(512, here)
    k_block = min(256, here)
    pair = k_len // k_block
    picture = jnp.arange(pics, dtype=jnp.int32)
    q_has = jnp.any(own_seg.reshape(-1, q_block, 1) == picture, axis=1)
    k_has = jnp.any(key_seg.reshape(-1, k_block, 1) == picture, axis=1)
    active = jnp.any(q_has[:, None, :] & k_has[None, :, :], axis=2)
    used = jnp.sum(active.astype(jnp.int32), axis=1, keepdims=True)
    counts = -(-jnp.max(used, axis=0) // pair)
    place = jnp.where(
        active,
        jnp.cumsum(active.astype(jnp.int32), axis=1) - 1,
        used + jnp.cumsum(1 - active.astype(jnp.int32), axis=1) - 1,
    )
    chunk_ids = jnp.arange(active.shape[1], dtype=jnp.int32)
    hit = place[:, :, None] == chunk_ids[None, None, :]
    indices = jnp.sum(jnp.where(hit, chunk_ids[None, :, None], 0), axis=1).reshape(-1)

    q_mask = jnp.concatenate(
        [
            jnp.where(own_seg[None, :] == picture[:, None], 0.0, MASKED),
            jnp.full((1, here), MASKED, F32),
        ],
        axis=0,
    )
    k_mask = jnp.concatenate(
        [(key_seg[None, :] == picture[:, None]), (key_seg >= pics)[None, :]], axis=0
    ).astype(BF)
    spare = AUG - (pics + 1) - 3
    k_added = jnp.concatenate(
        [k_mask, jnp.ones((3, k_len), BF), jnp.zeros((spare, k_len), BF)], axis=0
    )
    v_added = jnp.concatenate([jnp.ones((3, k_len), BF), jnp.zeros((AUG - 3, k_len), BF)], axis=0)

    grad_two = cotangent[0].astype(F32) * valid_col
    grad_mixed = grad_two.astype(BF)
    down_bias_part = jnp.sum(grad_mixed, axis=0, dtype=F32)
    later = [x_own, lax.ppermute(x_own, "tp", to_left)]
    prior = [x_own, lax.ppermute(x_own, "tp", to_right)]
    attn_parts = after(
        attn_parts,
        vectors,
        counts,
        indices,
        k_added,
        q_mask,
        down_bias_part,
        grad_mixed,
        later[1],
        prior[1],
    )
    share = query_weight.shape[1]
    all_biases = jnp.sum(
        attn_parts[:, share:]
        .reshape(n, -1)[:, : 3 * bias_piece.shape[0]]
        .reshape(n, 3, -1)
        .astype(F32),
        axis=1,
    )
    query_shift = all_biases[:, :cols].reshape(-1)
    value_shift = all_biases[:, cols : 2 * cols].reshape(-1)
    ring_order = (me - jnp.arange(n)) % n
    up_shift = jnp.take(all_biases[:, 2 * cols :], ring_order, axis=0).reshape(-1)
    wide_piece = jnp.concatenate([out_weight[0], up_weight[0]], axis=1)
    wide_slots = slots_along_tp(
        copy_after(wide_piece, attn_parts, up_shift, query_shift, value_shift), n
    )
    later[1], prior[1] = after(later[1], *wide_slots[1:]), after(prior[1], *wide_slots[1:])
    for _ in range(reach - 1):
        later.append(lax.ppermute(later[-1], "tp", to_left))
        prior.append(lax.ppermute(prior[-1], "tp", to_right))

    slot_count = 1 + len(slots)
    normed_all = norm_slot(x_own, gain_one, shift_one, 0, slot_count)
    for position, (j, use_later, use_prior) in enumerate(slots):
        if use_later and use_prior:
            tokens = jnp.where(me + j < n, later[j], prior[n - j])
        else:
            tokens = later[j] if use_later else prior[n - j]
        if min(j, n - j) == 1:
            normed_all = norm_slot(
                tokens, gain_one, shift_one, position + 1, slot_count, normed_all
            )
        else:
            normed_all = norm_slot(
                tokens, gain_one, shift_one, position + 1, slot_count, normed_all
            )

    def widen(body, added):
        body = body.reshape(heads, HEAD_DIM, body.shape[-1])
        added = jnp.broadcast_to(added, (heads, AUG, body.shape[-1]))
        return jnp.concatenate([body, added.astype(BF)], axis=1)

    attn_shard = jnp.concatenate(
        [attn_parts[o, :share, t * cols : (t + 1) * cols] for t in range(3) for o in range(n)],
        axis=1,
    )
    attn_full = lax.all_gather(attn_shard, "fsdp", axis=0, tiled=True)
    out_slots = jnp.take(jnp.stack([s[:, :cols] for s in wide_slots]), ring_order, axis=0)
    wide_shard = jnp.concatenate(
        [out_slots[o] for o in range(n)] + [s[:, cols:] for s in wide_slots], axis=1
    )
    wide_full = lax.all_gather(wide_shard, "fsdp", axis=0, tiled=True)
    out_full, up_full = wide_full[:, :hh], wide_full[:, hh:]

    query_full = attn_full[:, :hh]
    key_full = attn_full[:, hh : 2 * hh]
    value_full = attn_full[:, 2 * hh : 3 * hh]
    kv_full = attn_full[:, hh : 3 * hh]

    x = x_own.astype(F32)
    normed = normed_all[:here]
    queries = (
        (product("td,dc->ct", normed, query_full) + query_shift[:, None])
        * (scale * math.log2(math.e))
    ).astype(BF)
    first_down = copy_after(down_weight[0], later[-1], prior[-1])
    q_rest = jnp.zeros((AUG - (pics + 1), here), F32)
    q_aug = widen(queries, jnp.concatenate([q_mask, q_rest], axis=0))

    keys = product("td,dc->ct", normed_all, key_full).astype(BF)
    values = product("td,dc->ct", normed_all, value_full) + value_shift[:, None]
    k_aug = after(widen(keys, k_added))
    v_aug = after(widen(values.astype(BF), v_added))
    down_slots = slots_along_tp(first_down, n, k_aug, v_aug)
    group = 2 if heads % 4 == 0 else 1
    down_shard = jnp.concatenate(down_slots, axis=1)
    down_full = lax.all_gather(down_shard, "fsdp", axis=0, tiled=True)
    attended, log_total = attend(
        q_aug,
        k_aug,
        v_aug,
        valid[None, :],
        counts,
        indices,
        q_block,
        k_block,
        pair,
        group,
        0,
        1,
        down_shard,
    )
    flat = attended.reshape(hh, here)
    middle = x + (product("ct,dc->td", flat, out_full) + out_shift)

    two_hat, two_rstd = xhat_of(middle)
    normed_two = (two_hat * gain_two + shift_two).astype(BF)
    hidden = product("td,df->tf", normed_two, up_full) + up_shift
    active_units, gelu_pull = jax.vjp(gelu_tanh, hidden)
    active_units = active_units.astype(BF)

    down_grad = product("td,tf->df", grad_mixed, active_units).astype(BF)
    down_scattered = lax.psum_scatter(down_grad, "fsdp", scatter_dimension=0, tiled=True)
    back_mixed = after(grad_mixed, down_grad)
    grad_hidden = gelu_pull(product("td,df->tf", back_mixed, down_full))[0].astype(BF)
    up_bias_part = jnp.sum(grad_hidden, axis=0, dtype=F32)
    up_grad = product("td,tf->df", normed_two, grad_hidden).astype(BF)
    grad_normed_two = product("tf,df->td", grad_hidden, up_full)
    grad_middle, gain_two_part, shift_two_part = norm_back(
        grad_normed_two, two_hat, two_rstd, gain_two
    )
    grad_middle = grad_two + grad_middle
    grad_branch = grad_middle.astype(BF)
    out_bias_part = jnp.sum(grad_branch, axis=0, dtype=F32)
    out_grad = product("td,ct->dc", grad_branch, flat).astype(BF)
    up_scattered = lax.psum_scatter(up_grad, "fsdp", scatter_dimension=0, tiled=True)

    grad_attended = product("td,dc->ct", grad_branch, out_full).astype(BF)
    grad_attended = grad_attended * valid.astype(BF)
    grad_heads = grad_attended.reshape(heads, HEAD_DIM, here)
    delta = jnp.sum(grad_heads.astype(F32) * attended.astype(F32), axis=1)
    g_added = jnp.concatenate(
        [
            jnp.moveaxis(split3(-delta), 0, 1),
            jnp.zeros((heads, AUG - 3, here), F32),
        ],
        axis=1,
    )
    g_aug = widen(grad_attended, g_added)
    q_added = jnp.concatenate(
        [
            jnp.broadcast_to(q_mask, (heads, pics + 1, here)),
            jnp.moveaxis(split3(-log_total[:, 0]), 0, 1),
            jnp.zeros((heads, spare, here), F32),
        ],
        axis=1,
    )
    q_aug_back = widen(queries, q_added)
    def back_part(part, before, *earlier):
        return attend_back(
            q_aug_back,
            k_aug,
            v_aug,
            g_aug,
            counts,
            indices,
            q_block,
            k_block,
            pair,
            group,
            part,
            2,
            before,
            *earlier,
        )

    parts = back_part(0, (), up_grad, out_grad)
    down_scattered = after(down_scattered, parts[0])
    down_moved = [
        lax.ppermute(
            down_scattered[:, s * units : (s + 1) * units],
            "tp",
            [(i, (i - s) % n) for i in range(n)],
        )
        for s in range(1, n)
    ]
    dq, dkv = back_part(1, parts, down_scattered)
    down_moved = [after(moved, dq) for moved in down_moved]
    dq, dkv = dq.reshape(hh, -1), dkv.reshape(2 * hh, -1)

    def share_of(position, dkv):
        part = slice(position * here, (position + 1) * here)
        return product("ct,dc->td", dkv[:, part], kv_full)

    to_later = [None] * (reach + 1)
    to_prior = [None] * (reach + 1)

    def send_shares(distance, dkv, sides="both"):
        for i, (j, use_later, use_prior) in enumerate(slots):
            to_right_here = use_later and j == distance and sides != "prior"
            to_left_here = use_prior and n - j == distance and sides != "later"
            if not (to_right_here or to_left_here):
                continue
            part = share_of(i + 1, dkv).astype(BF)
            zero = jnp.zeros_like(part)
            if to_right_here:
                to_later[j] = jnp.where(me + j < n, part, zero)
            if to_left_here:
                to_prior[n - j] = jnp.where(me + j >= n, part, zero)

    def joined(moving, share_here):
        return (moving.astype(F32) + share_here.astype(F32)).astype(BF)

    send_shares(reach, dkv)
    moving_right = lax.ppermute(to_later[reach], "tp", to_right)
    moving_left = lax.ppermute(to_prior[reach], "tp", to_left)
    dkv = after(dkv, to_later[reach], to_prior[reach], *down_moved)
    query_grad = product("td,ct->dc", normed, dq).astype(BF)
    kv_grad = product("td,ct->dc", normed_all, dkv).astype(BF)
    gates = (kv_grad, query_grad)
    if reach > 1:
        dkv = after(dkv, *gates)
        for distance in reversed(range(2, reach)):
            send_shares(distance, dkv)
        gates = (*gates, moving_right, moving_left)
    attn_grad = jnp.concatenate([query_grad, kv_grad, after(out_grad, *gates)], axis=1)
    attn_scattered = lax.psum_scatter(attn_grad, "fsdp", scatter_dimension=0, tiled=True)
    dkv, up_scattered = after(dkv, attn_grad), after(up_scattered, attn_grad)
    up_moved = [
        lax.ppermute(
            up_scattered[:, s * units : (s + 1) * units],
            "tp",
            [(i, (i - s) % n) for i in range(n)],
        )
        for s in range(1, n)
    ]
    for distance in reversed(range(2, reach)):
        moving_right = lax.ppermute(joined(moving_right, to_later[distance]), "tp", to_right)
        moving_left = lax.ppermute(joined(moving_left, to_prior[distance]), "tp", to_left)
    if reach > 1:
        send_shares(1, dkv, "later")
        moving_right = joined(moving_right, to_later[1])
        dkv = after(dkv, moving_right, *up_moved[:1])
        dq = after(dq, moving_right, *up_moved[1:2])
        moving_right = lax.ppermute(moving_right, "tp", to_right)
    own_share = share_of(0, dkv) + product("ct,dc->td", dq, query_full)
    if reach > 1:
        dkv = after(dkv, own_share)
        send_shares(1, dkv, "prior")
        moving_right = after(moving_right, to_prior[1])
        moving_left = lax.ppermute(joined(moving_left, to_prior[1]), "tp", to_left)
    last_sent = [t for t in (own_share, to_prior[1], *up_moved) if t is not None]
    grad_normed = own_share + moving_right.astype(F32) + moving_left.astype(F32)

    one_hat, one_rstd = xhat_of(x)
    grad_x, gain_one_part, shift_one_part = norm_back(grad_normed, one_hat, one_rstd, gain_one)
    input_grad = grad_middle + grad_x

    query_bias_part = jnp.sum(dq, axis=1, dtype=F32)
    value_bias_part = jnp.sum(dkv[hh:], axis=1, dtype=F32)
    vector_part = jnp.concatenate(
        [
            gain_one_part,
            shift_one_part,
            out_bias_part,
            gain_two_part,
            shift_two_part,
            down_bias_part,
        ]
    )
    up_bias_parts = jnp.take(up_bias_part.reshape(n, units), ring_order, axis=0).reshape(-1)
    small = jnp.concatenate([query_bias_part, value_bias_part, up_bias_parts, vector_part])

    def sum_over(value, axis):
        count = lax.axis_size(axis)
        if count & (count - 1):
            return lax.psum(value, axis)
        bit = 1
        while bit < count:
            value = value + lax.ppermute(value, axis, [(i, i ^ bit) for i in range(count)])
            bit *= 2
        return value

    def summed(scattered, moved):
        return sum((m.astype(F32) for m in moved), scattered[:, :units].astype(F32))

    down_weight_grad = summed(down_scattered, down_moved)
    up_weight_grad = summed(up_scattered, up_moved)
    attn_owned = by_owner(after(attn_scattered, *last_sent), n, 4)
    small = after(small, attn_owned)
    small = sum_over(sum_over(small, "tp"), "fsdp")
    attn_out = lax.psum_scatter(attn_owned, "tp", scatter_dimension=0, tiled=True).astype(F32)
    mixed = product("tf,df->td", after(active_units, attn_owned), down_full) + down_shift
    activations_out = ((middle + mixed) * valid_col).astype(BF)

    bias_size = (2 * cols + units) * n
    query_bias_grad, value_bias_grad, up_bias_grad = (
        lax.dynamic_slice_in_dim(small, start + me * size, size, 0)
        for start, size in ((0, cols), (hh, cols), (2 * hh, units))
    )
    own_vectors = lax.dynamic_slice_in_dim(
        small[bias_size:].reshape(6, width), lax.axis_index("fsdp") * share, share, 1
    )
    return (
        activations_out[None],
        input_grad[None],
        own_vectors[0:1],
        own_vectors[1:2],
        attn_out[None, :, :cols],
        query_bias_grad[None],
        attn_out[None, :, cols : 2 * cols],
        attn_out[None, :, 2 * cols : 3 * cols],
        value_bias_grad[None],
        attn_out[None, :, 3 * cols :],
        own_vectors[2:3],
        own_vectors[3:4],
        own_vectors[4:5],
        up_weight_grad[None],
        up_bias_grad[None],
        down_weight_grad[None],
        own_vectors[5:6],
    )


def solution(mesh):
    token = P("fsdp", "tp", None)
    vector, shift, matrix = P(None, "fsdp"), P(None, "tp"), P(None, "fsdp", "tp")
    in_specs = (
        token,
        P("fsdp", None),
        token,
        vector,
        vector,
        matrix,
        shift,
        matrix,
        matrix,
        shift,
        matrix,
        vector,
        vector,
        vector,
        matrix,
        shift,
        matrix,
        vector,
    )
    out_specs = (
        token,
        token,
        vector,
        vector,
        matrix,
        shift,
        matrix,
        matrix,
        shift,
        matrix,
        vector,
        vector,
        vector,
        matrix,
        shift,
        matrix,
        vector,
    )
    return jax.shard_map(local, mesh=mesh, in_specs=in_specs, out_specs=out_specs, check_vma=False)
```
